32 devices in a mesh: parts: 2 (over x), serve: 8 (over z, y), tensor: 2 (over core).
Axes of the slice: x: 2, y: 2, z: 4, core: 2. Of those that a mesh axis runs over, the one named last changes fastest.
Arguments:
- hidden: bfloat16 [2, 512, 8192], P(None, ('parts', 'serve')), parts along dimension 1, may hold values from -6 to 6
- query: bfloat16 [2, 512, 4096], P(None, ('parts', 'serve'), 'tensor'), parts along dimension 1, may hold values from -48 to 48
- kv_weight: bfloat16 [8192, 1024], P(None, 'tensor'), may hold values from -0.0625 to 0.0625
- down_store: bfloat16 [2, 4096, 8192], P('tensor', None, 'serve'), may hold values from -0.0625 to 0.0625
- up_store: bfloat16 [2, 512, 4096], P('tensor', 'serve'), may hold values from -1.5 to 1.5
- kv_cache: bfloat16 [512, 64, 1024], P(('parts', 'serve'), None, 'tensor'), parts along dimension 0, may hold values from -6 to 6
- cache_len: int32 [512], P(('parts', 'serve')), parts along dimension 0, may hold values from 2 to 62, as said below
- block_adapter: int32 [4], P('parts'), parts along dimension 0, may hold values from 0 to 255
- block_fill: int32 [4], P('parts'), parts along dimension 0, may hold values from 1 to 128
Outputs:
- new_kv: bfloat16 [2, 512, 1024], P(None, ('parts', 'serve'), 'tensor'), parts along dimension 1
- attn: bfloat16 [2, 512, 4096], P(None, ('parts', 'serve'), 'tensor'), parts along dimension 1
The draws below stay inside these ranges and needn't reach their ends.
There are 2 independent parts, one for each index of `parts`. The reference program is written for one: setup_inputs(seed, part) draws one part's arguments, and reference() takes and returns one part's arrays. A program takes and returns all parts, laid end to end along the dimension named above; an argument that names none is the same for every part. Nothing has to cross between parts.
Inputs may be any that keep to these rules, and one draw needn't show every extreme that they name: `cache_len`: some row has exactly 62 positions in every draw.
All inputs are finite; a program needn't handle non-finite values.
Results may differ from the reference program's by a relative error of at most 0.0076.
Values may be sent and summed in bfloat16 or wider, within the bound.
No kernel may reach another device: no remote copies, remote signals or barrier semaphores. Data moves between devices by JAX's collectives and lax.ppermute only.
A program may use at most 64 MiB of HBM per device.

```python
import math
import jax
import jax.numpy as jnp
import numpy as np
from jax import lax

D = 8192
QUERY_HEADS = 32
KEY_VALUE_HEADS = 4
HEAD_SIZE = 128
RANK = 16
NA = 256
CACHE_LENGTH = 64
BLK = 128
STEPS = 2
REQUEST_ROWS = 256
NBLK = 2
KVC = 1024
QUERY_WIDTH = 4096


def draw_kv_cache(key, part):
    key = jax.random.fold_in(key, 3)
    values = jnp.clip(jax.random.normal(key, (REQUEST_ROWS, CACHE_LENGTH, KVC)), -6.0, 6.0)
    return values.astype(jnp.bfloat16)


def draw_query(key, part):
    key = jax.random.fold_in(key, 5)
    values = jnp.clip(jax.random.normal(key, (STEPS, REQUEST_ROWS, QUERY_WIDTH)), -6.0, 6.0)
    return values.astype(jnp.bfloat16)


def draw_cache_len(key, part):
    key = jax.random.fold_in(key, 7)
    main_key, pick_key = jax.random.split(key)
    lengths = jax.random.randint(main_key, (REQUEST_ROWS,), 2, CACHE_LENGTH - STEPS + 1)
    longest = jax.random.randint(pick_key, (), 0, REQUEST_ROWS)
    return jnp.where(jnp.arange(REQUEST_ROWS) == longest, CACHE_LENGTH - STEPS, lengths).astype(jnp.int32)


def spiked(values, stream_key, source, target, parts, factor):
    owner, partner = [(jnp.arange(values.shape[axis_at]) // (values.shape[axis_at] // parts)).reshape([-1 if axis == axis_at else 1 for axis in range(values.ndim)]) for axis_at in (source, target)]
    chosen = jax.random.permutation(stream_key, parts)[partner]
    strong = (owner == chosen) | (owner == (partner + parts // 2) % parts)
    return jnp.where(strong, factor * values, values)


def block_levels(stream_key, shape, shards, smallest, largest):
    def one(dim, blocks):
        steps = jax.random.uniform(jax.random.fold_in(jax.random.fold_in(stream_key, 6), dim), (blocks,), jnp.float32, smallest / len(shards), largest / len(shards))
        return jnp.repeat(jnp.exp(steps), shape[dim] // blocks).reshape((-1,) + (1,) * (len(shape) - dim - 1))

    level = one(*shards[0])
    for cut in shards[1:]:
        level = level * one(*cut)
    return level


def rank_table(number_of, slope):
    portions = [(1 << 20) // math.isqrt(rank ** slope) + 1 for rank in range(1, number_of + 1)]
    deviation = 1 + sum(portions) // (1 << 30)
    return np.cumsum(np.array([max(1, weight // deviation) for weight in portions]))


def skewed_ids(own_key, extent, amount, slope):
    grid = rank_table(amount, slope)
    ticket = jax.random.randint(jax.random.fold_in(own_key, 1), extent, 0, int(grid[amount - 1]))
    grade = jnp.searchsorted(jnp.asarray(grid, jnp.int32), ticket, side="right")
    return jax.random.permutation(jax.random.fold_in(own_key, 2), amount)[grade].astype(jnp.int32)


def normal_values(stream_key, dims, width, most, shards=(), held_as=jnp.bfloat16):
    loudness = block_levels(stream_key, dims, shards, -0.22, 0.18) if shards else 1.0
    result = jax.random.normal(stream_key, dims, jnp.float32) * width * loudness
    return jnp.minimum(jnp.maximum(result, -most), most).astype(held_as)


def gaussian_with(stream_key, shape, width, bound, shards, heavy, kind=jnp.bfloat16):
    drawn = width * jax.random.normal(stream_key, shape, jnp.float32)
    if shards:
        drawn = drawn * block_levels(stream_key, shape, shards, -0.22, 0.18)
    return jnp.clip(spiked(drawn, jax.random.fold_in(stream_key, 3), *heavy), -bound, bound).astype(kind)


def setup_inputs(seed: int = 0, part: int = 0) -> dict:
    keys = jax.random.split(jax.random.key(seed), 10)
    part_keys = jax.random.split(jax.random.fold_in(keys[9], part), 10)
    hidden = gaussian_with(part_keys[0], (STEPS, REQUEST_ROWS, D), 1.0, 6.0, ((1, 8),), (2, 1, 8, 2.0))
    query = draw_query(jax.random.fold_in(jax.random.fold_in(keys[9], part), 71), part)
    kv_weight = normal_values(keys[2], (D, KVC), D ** -0.5, 0.0625, ((1, 2),))
    down_store = normal_values(keys[3], (2, NA * RANK, D), D ** -0.5, 0.0625, ((0, 2), (2, 8)))
    up_store = normal_values(keys[4], (2, KVC // 2, NA * RANK), RANK ** -0.5, 1.5, ((0, 2), (1, 8)))
    kv_cache = draw_kv_cache(jax.random.fold_in(jax.random.fold_in(keys[9], part), 71), part)
    cache_len = draw_cache_len(jax.random.fold_in(jax.random.fold_in(keys[9], part), 71), part)
    block_adapter = skewed_ids(part_keys[7], (NBLK,), NA, 2)
    block_fill = jax.random.randint(part_keys[8], (NBLK,), 1, BLK + 1).astype(jnp.int32)
    return {"hidden": hidden, "query": query, "kv_weight": kv_weight, "down_store": down_store, "up_store": up_store, "kv_cache": kv_cache, "cache_len": cache_len, "block_adapter": block_adapter, "block_fill": block_fill}


ADAPTER_SCALE = 2.0


def attend_rows(items):
    row_queries, cached_row_block, lengths, latest_rows = items
    count_of_rows = row_queries.shape[0]
    head_queries = row_queries.astype(jnp.float32).reshape(count_of_rows, KEY_VALUE_HEADS, QUERY_HEADS // KEY_VALUE_HEADS, HEAD_SIZE)
    matched_pairs = cached_row_block.astype(jnp.float32).reshape(count_of_rows, CACHE_LENGTH, KEY_VALUE_HEADS, 2, HEAD_SIZE)
    latest_entries = latest_rows.astype(jnp.float32).reshape(count_of_rows, -1, KEY_VALUE_HEADS, 2, HEAD_SIZE)
    score_scale = HEAD_SIZE ** -0.5
    scores = jnp.einsum('nhgd,nphd->nhgp', head_queries, matched_pairs[:, :, :, 0]) * score_scale
    valid = jnp.arange(CACHE_LENGTH)[None, :] < lengths[:, None]
    scores = jnp.where(valid[:, None, None, :], scores, -jnp.inf)
    new_scores = jnp.einsum('nhgd,nthd->nhgt', head_queries, latest_entries[:, :, :, 0]) * score_scale
    highest = jnp.maximum(jnp.max(scores, axis=-1), jnp.max(new_scores, axis=-1))
    cache_exp = jnp.exp(scores - highest[..., None])
    new_exp = jnp.exp(new_scores - highest[..., None])
    denominator = jnp.sum(cache_exp, axis=-1) + jnp.sum(new_exp, axis=-1)
    cache_weight = (cache_exp / denominator[..., None]).astype(jnp.bfloat16).astype(jnp.float32)
    new_weight = (new_exp / denominator[..., None]).astype(jnp.bfloat16).astype(jnp.float32)
    mixed = jnp.einsum('nhgp,nphd->nhgd', cache_weight, matched_pairs[:, :, :, 1])
    mixed = mixed + jnp.einsum('nhgt,nthd->nhgd', new_weight, latest_entries[:, :, :, 1])
    return mixed.reshape(count_of_rows, QUERY_HEADS * HEAD_SIZE)


def reference(hidden, query, kv_weight, down_store, up_store, kv_cache, cache_len, block_adapter, block_fill):
    row_ids = jnp.arange(REQUEST_ROWS)
    block_ids = row_ids // BLK
    live = ((row_ids % BLK) < block_fill[block_ids]).astype(jnp.float32)
    kinds = (jnp.arange(KVC) // HEAD_SIZE) % 2
    down_all = down_store.reshape(2, NA, RANK, D)
    up_all = up_store.reshape(KVC, NA, RANK)
    down_chosen = down_all[:, block_adapter].astype(jnp.float32)
    up_chosen = up_all[:, block_adapter, :].astype(jnp.float32)
    group_size = math.gcd(REQUEST_ROWS, 64)
    group_count = REQUEST_ROWS // group_size
    fresh_list = []
    attn_list = []
    for step_index in range(STEPS):
        states = hidden[step_index]
        base = jnp.dot(states, kv_weight, preferred_element_type=jnp.float32)
        grouped_states = states.astype(jnp.float32).reshape(NBLK, BLK, D)
        low_rank = jnp.einsum('bnd,kbrd->bnkr', grouped_states, down_chosen).reshape(REQUEST_ROWS, 2, RANK)
        shrunk = (low_rank * live[:, None, None]).astype(jnp.bfloat16).astype(jnp.float32)
        shrunk_blocks = shrunk.reshape(NBLK, BLK, 2, RANK)
        key_delta = jnp.einsum('bnr,cbr->bnc', shrunk_blocks[:, :, 0], up_chosen).reshape(REQUEST_ROWS, KVC)
        value_delta = jnp.einsum('bnr,cbr->bnc', shrunk_blocks[:, :, 1], up_chosen).reshape(REQUEST_ROWS, KVC)
        delta = jnp.where(kinds[None, :] == 0, key_delta, value_delta)
        new_kv = (live[:, None] * (base + ADAPTER_SCALE * delta)).astype(jnp.bfloat16)
        fresh_list.append(new_kv)
        recent_all = jnp.stack(fresh_list, axis=1)
        packed = (query[step_index].reshape(group_count, group_size, QUERY_HEADS * HEAD_SIZE),
                  kv_cache.reshape(group_count, group_size, CACHE_LENGTH, KVC),
                  cache_len.reshape(group_count, group_size),
                  recent_all.reshape(group_count, group_size, len(fresh_list), KVC))
        mixed = lax.map(attend_rows, packed).reshape(REQUEST_ROWS, QUERY_HEADS * HEAD_SIZE)
        attn_list.append((mixed * live[:, None]).astype(jnp.bfloat16))
    return jnp.stack(fresh_list), jnp.stack(attn_list)
```

```python
import functools
import math

import jax
import jax.numpy as jnp
from jax import lax
from jax.experimental import pallas as pl
from jax.experimental.pallas import tpu as pltpu
from jax.sharding import PartitionSpec as P

HEAD = 128
RANK = 16
BLK = 128
LANES = 128
ADAPTER_SCALE = 2.0
ROW_GROUP = 8
EXP_SCALE = HEAD ** (-0.5) * math.log2(math.e)

HBM = pl.BlockSpec(memory_space=pl.ANY)
SMEM = pl.BlockSpec(memory_space=pltpu.SMEM)
VMEM = pl.BlockSpec(memory_space=pltpu.VMEM)


def dot_t(a, b):
    return lax.dot_general(a, b, (((1,), (1,)), ((), ())), preferred_element_type=jnp.float32)


def place():
    return lax.axis_index("serve")


def pack_kernel(groups, size, adapter_ref, down_ref, up_ref, *rest):
    out_refs, (window, down_sem, up_sem) = rest[:-3], rest[-3:]
    first = lax.axis_index("serve") // size if groups == 2 else 0
    width = down_ref.shape[2]
    cols = up_ref.shape[1]
    copies = []
    starts = []
    for k in range(groups):
        adapter = adapter_ref[lax.rem(first + k, groups)]
        out = out_refs[k] if groups == 2 else out_refs[0].at[k]
        down = pltpu.make_async_copy(
            down_ref.at[0, pl.ds(pl.multiple_of(adapter * RANK, RANK), RANK), :],
            out.at[:, pl.ds(0, width)],
            down_sem.at[k],
        )
        lane = adapter * RANK // LANES * LANES
        up = pltpu.make_async_copy(
            up_ref.at[0, :, pl.ds(pl.multiple_of(lane, LANES), LANES)], window.at[k], up_sem.at[k]
        )
        up.start()
        down.start()
        copies.append((down, up, out))
        starts.append(adapter * RANK - lane)
    repeat = lax.broadcasted_iota(jnp.int32, (LANES, cols), 0) % cols
    spread = (repeat == lax.broadcasted_iota(jnp.int32, (LANES, cols), 1)).astype(jnp.bfloat16)
    ranks = lax.broadcasted_iota(jnp.int32, (RANK, LANES), 0)
    lanes = lax.broadcasted_iota(jnp.int32, (RANK, LANES), 1)
    for k in range(groups):
        down, up, out = copies[k]
        up.wait()
        chosen = (lanes == ranks + starts[k]).astype(jnp.bfloat16)
        repeated = jnp.dot(spread, window[k], preferred_element_type=jnp.float32).astype(jnp.bfloat16)
        out[:, width : width + LANES] = dot_t(chosen, repeated).astype(jnp.bfloat16)
    for down, _, _ in copies:
        down.wait()


def pack(block_adapter, down_store, up_store, groups, size):
    width = down_store.shape[2] + LANES
    cols = up_store.shape[1]
    if groups == 2:
        out_shape = [jax.ShapeDtypeStruct((RANK, width), jnp.bfloat16)] * 2
        out_specs = [VMEM] * 2
    else:
        out_shape = [jax.ShapeDtypeStruct((groups, RANK, width), jnp.bfloat16)]
        out_specs = [VMEM]
    return pl.pallas_call(
        functools.partial(pack_kernel, groups, size),
        out_shape=out_shape,
        in_specs=[SMEM, HBM, HBM],
        out_specs=out_specs,
        scratch_shapes=[
            pltpu.VMEM((groups, cols, LANES), jnp.bfloat16),
            pltpu.SemaphoreType.DMA((groups,)),
            pltpu.SemaphoreType.DMA((groups,)),
        ],
        name="pack",
    )(block_adapter, down_store, up_store)


def base_kernel(hidden_ref, weight_ref, base_ref):
    steps, rows, width = hidden_ref.shape

    @pl.when(pl.program_id(0) == 0)
    def _():
        base_ref[...] = jnp.zeros_like(base_ref)

    states = hidden_ref[...].reshape(steps * rows, width)
    base_ref[...] += jnp.dot(states, weight_ref[...], preferred_element_type=jnp.float32)


def base_projection(hidden, kv_weight):
    steps, rows, width = hidden.shape
    cols = kv_weight.shape[1]
    chunk = 1024
    return pl.pallas_call(
        base_kernel,
        grid=(width // chunk,),
        out_shape=jax.ShapeDtypeStruct((steps * rows, cols), jnp.float32),
        in_specs=[
            pl.BlockSpec((steps, rows, chunk), lambda i: (0, 0, i)),
            pl.BlockSpec((chunk, cols), lambda i: (i, 0)),
        ],
        out_specs=pl.BlockSpec((steps * rows, cols), lambda i: (0, 0)),
        cost_estimate=pl.CostEstimate(
            flops=2 * steps * rows * width * cols,
            bytes_accessed=2 * width * cols + 2 * steps * rows * width,
            transcendentals=0,
        ),
        name="base",
    )(hidden, kv_weight)


def cache_kernel(len_ref, query_ref, cache_ref, mix_ref, sum_ref, max_ref):
    steps, rows, _ = query_ref.shape
    positions = cache_ref.shape[1]
    kv_heads = cache_ref.shape[2] // (2 * HEAD)
    share = query_ref.shape[2] // (kv_heads * HEAD)
    wide = ROW_GROUP * positions
    lanes = lax.broadcasted_iota(jnp.int32, (ROW_GROUP, wide), 1)
    subs = lax.broadcasted_iota(jnp.int32, (ROW_GROUP, wide), 0)
    ones = jnp.ones((wide, HEAD), jnp.bfloat16)

    def pair(p, carry):
        first = pl.multiple_of(p * 2 * ROW_GROUP, 2 * ROW_GROUP)
        for half in range(2):
            lengths = jnp.zeros((ROW_GROUP, wide), jnp.int32)
            for r in range(ROW_GROUP):
                lengths = jnp.where(subs == r, len_ref[first + half * ROW_GROUP + r], lengths)
            start = subs * positions
            bias = jnp.where((lanes >= start) & (lanes < start + lengths), 0.0, -jnp.inf)
            own = pl.ds(pl.multiple_of(first + half * ROW_GROUP, ROW_GROUP), ROW_GROUP)
            for g in range(kv_heads):
                stored = cache_ref[own, :, g * 2 * HEAD : (g + 1) * 2 * HEAD].reshape(wide, 2 * HEAD)
                parts = []
                for s in range(steps):
                    for j in range(share):
                        at = (g * share + j) * HEAD
                        both = query_ref[s, pl.ds(first, 2 * ROW_GROUP), at : at + HEAD]
                        both = both.astype(jnp.float32)
                        parts.append(both[half * ROW_GROUP : (half + 1) * ROW_GROUP])
                stacked = jnp.concatenate(parts, axis=0).astype(jnp.bfloat16)
                scores = dot_t(stacked, stored[:, :HEAD]).reshape(steps * share, ROW_GROUP, wide)
                scores = scores + bias[None]
                highest = jnp.max(scores, axis=-1, keepdims=True)
                weights = jnp.exp2((scores - highest) * EXP_SCALE).reshape(-1, wide).astype(jnp.bfloat16)
                values = jnp.concatenate([stored[:, HEAD:], ones], axis=1)
                mixed = jnp.dot(weights, values, preferred_element_type=jnp.float32)
                mixed = mixed.reshape(steps, share, ROW_GROUP, 2 * HEAD)
                mix_ref[g, :, :, own, :] = mixed[..., :HEAD]
                sum_ref[g, :, :, own, :] = mixed[..., HEAD:]
                max_ref[g, :, :, own, :] = jnp.broadcast_to(
                    highest.reshape(steps, share, ROW_GROUP, 1), (steps, share, ROW_GROUP, HEAD)
                )
        return carry

    lax.fori_loop(0, rows // (2 * ROW_GROUP), pair, 0)


def cache_attention(cache_len, query, kv_cache):
    steps, rows, heads_width = query.shape
    kv_heads = kv_cache.shape[2] // (2 * HEAD)
    share = heads_width // (kv_heads * HEAD)
    shape = jax.ShapeDtypeStruct((kv_heads, steps, share, rows, HEAD), jnp.float32)
    return pl.pallas_call(
        cache_kernel,
        out_shape=[shape] * 3,
        in_specs=[SMEM, VMEM, VMEM],
        out_specs=[VMEM] * 3,
        cost_estimate=pl.CostEstimate(
            flops=2 * 2 * steps * heads_width * rows * ROW_GROUP * kv_cache.shape[1],
            bytes_accessed=2 * kv_cache.size,
            transcendentals=0,
        ),
        name="cached",
    )(cache_len, query, kv_cache)


def shrink_kernel(groups, size, fill_ref, hidden_ref, own_ref, *rest):
    peer_refs, (low_ref, up_ref) = rest[:-2], rest[-2:]
    steps, rows, _ = hidden_ref.shape
    width = own_ref.shape[2] - LANES
    me = lax.axis_index("serve")
    block = me // size
    mine = lax.rem(me, size)
    first = block if groups == 2 else 0
    total = jnp.zeros((steps * rows, RANK), jnp.float32)
    for d, ref in enumerate((own_ref,) + tuple(peer_refs)):
        for e in range(groups):
            source = lax.rem(first + e, groups) * size + (mine ^ d)
            states = hidden_ref[:, :, pl.ds(pl.multiple_of(source * width, LANES), width)]
            factors = ref[e]
            total += dot_t(states.reshape(steps * rows, width), factors[:, :width])
            up_ref[source] = factors[:, width:]
    row = lax.broadcasted_iota(jnp.int32, (steps * rows, RANK), 0) % rows + mine * rows
    low_ref[...] = jnp.where(row < fill_ref[block], total, 0.0).astype(jnp.bfloat16)


def shrink(block_fill, hidden, parts, groups, size):
    steps, rows, _ = hidden.shape
    return pl.pallas_call(
        functools.partial(shrink_kernel, groups, size),
        out_shape=[
            jax.ShapeDtypeStruct((steps * rows, RANK), jnp.bfloat16),
            jax.ShapeDtypeStruct((groups * size, RANK, LANES), jnp.bfloat16),
        ],
        in_specs=[SMEM, VMEM] + [VMEM] * len(parts),
        out_specs=[VMEM] * 2,
        name="shrink",
    )(block_fill, hidden, *parts)


def final_kernel(
    size, cols, fill_ref, low_ref, other_ref, up_ref, base_ref, query_ref, mix_ref, sum_ref, max_ref,
    new_ref, attn_ref,
):
    steps, rows, _ = query_ref.shape
    kv_heads, _, share = mix_ref.shape[:3]
    total = steps * rows
    me = lax.axis_index("serve")
    fill = fill_ref[me // size]
    first = lax.rem(me, size) * rows
    live = (lax.broadcasted_iota(jnp.int32, (total, HEAD), 0) % rows + first < fill).astype(jnp.float32)
    core = lax.axis_index("tensor")
    keys_low = jnp.where(core == 0, low_ref[...], other_ref[...])
    values_low = jnp.where(core == 0, other_ref[...], low_ref[...])
    lane = lax.broadcasted_iota(jnp.int32, (RANK, LANES), 1)
    each = LANES // cols
    query_row = lax.broadcasted_iota(jnp.int32, (total, total), 0)
    key_row = lax.broadcasted_iota(jnp.int32, (total, total), 1)
    seen = (query_row % rows == key_row % rows) & (key_row // rows <= query_row // rows)
    bias = jnp.where(seen, 0.0, -jnp.inf).reshape(steps, 1, rows, total)
    ones = jnp.ones((total, HEAD), jnp.bfloat16)
    live_row = live[:rows]
    for g in range(kv_heads):
        fresh = []
        for kind, low in enumerate((keys_low, values_low)):
            tile = g * 2 + kind
            up = up_ref[tile * each]
            for k in range(1, each):
                up = jnp.where(lane // cols == k, up_ref[tile * each + k], up)
            delta = jnp.dot(low, up, preferred_element_type=jnp.float32)
            at = slice(tile * HEAD, (tile + 1) * HEAD)
            value = (live * (base_ref[:, at] + ADAPTER_SCALE * delta)).astype(jnp.bfloat16)
            new_ref[:, :, at] = value.reshape(steps, rows, HEAD)
            fresh.append(value)
        for s in range(steps):
            queries = jnp.concatenate(
                [query_ref[s, :, (g * share + j) * HEAD : (g * share + j + 1) * HEAD] for j in range(share)],
                axis=0,
            )
            scores = dot_t(queries, fresh[0]).reshape(share, rows, total) + bias[s]
            cached_max = max_ref[g, s]
            highest = jnp.maximum(cached_max, jnp.max(scores, axis=-1, keepdims=True))
            weights = jnp.exp2((scores - highest[:, :, :total]) * EXP_SCALE)
            keep = jnp.exp2((cached_max - highest) * EXP_SCALE)
            values = jnp.concatenate([fresh[1], ones], axis=1)
            mixed = jnp.dot(
                weights.reshape(-1, total).astype(jnp.bfloat16), values, preferred_element_type=jnp.float32
            ).reshape(share, rows, 2 * HEAD)
            top = mix_ref[g, s] * keep + mixed[..., :HEAD]
            bottom = sum_ref[g, s] * keep + mixed[..., HEAD:]
            result = (top / bottom * live_row[None]).astype(jnp.bfloat16)
            for j in range(share):
                attn_ref[s, :, (g * share + j) * HEAD : (g * share + j + 1) * HEAD] = result[j]


def finish(block_fill, low, other, up, base, query, cached, size, cols):
    steps, rows, _ = query.shape
    return pl.pallas_call(
        functools.partial(final_kernel, size, cols),
        out_shape=[
            jax.ShapeDtypeStruct((steps, rows, base.shape[1]), jnp.bfloat16),
            jax.ShapeDtypeStruct(query.shape, jnp.bfloat16),
        ],
        in_specs=[SMEM] + [VMEM] * 8,
        out_specs=[VMEM] * 2,
        name="finish",
    )(block_fill, low, other, up, base, query, *cached)


def local(
    hidden, query, kv_weight, down_store, up_store, kv_cache, cache_len, block_adapter, block_fill
):
    serve = lax.axis_size("serve")
    rows = hidden.shape[1]
    size = BLK // rows
    groups = serve // size
    packed = pack(block_adapter, down_store, up_store, groups, size)
    if groups == 2:
        own, other = packed
        swap = [(i, (i + size) % serve) for i in range(serve)]
        arrived = jnp.stack([own, lax.ppermute(other, "serve", swap)])
    else:
        same = [[g * size + j for g in range(groups)] for j in range(size)]
        arrived = lax.all_to_all(packed[0], "serve", 0, 0, axis_index_groups=same, tiled=True)
    parts = [arrived]
    for d in range(1, size):
        parts.append(lax.ppermute(arrived, "serve", [(i, i ^ d) for i in range(serve)]))
    base = base_projection(hidden, kv_weight)
    cached = cache_attention(cache_len, query, kv_cache)
    low, up = shrink(block_fill, hidden, parts, groups, size)
    other_low = lax.ppermute(low, "tensor", [(0, 1), (1, 0)])
    return tuple(finish(block_fill, low, other_low, up, base, query, cached, size, up_store.shape[1]))


def solution(mesh):
    in_specs = (
        P(None, ("parts", "serve"), None),
        P(None, ("parts", "serve"), "tensor"),
        P(None, "tensor"),
        P("tensor", None, "serve"),
        P("tensor", "serve", None),
        P(("parts", "serve"), None, "tensor"),
        P(("parts", "serve")),
        P("parts"),
        P("parts"),
    )
    out_specs = (P(None, ("parts", "serve"), "tensor"), P(None, ("parts", "serve"), "tensor"))
    return jax.shard_map(local, mesh=mesh, in_specs=in_specs, out_specs=out_specs, check_vma=False)
```

```python
import functools
import math

import jax
import jax.numpy as jnp
from jax import lax
from jax.experimental import pallas as pl
from jax.experimental.pallas import tpu as pltpu
from jax.sharding import PartitionSpec as P

HEAD = 128
RANK = 16
BLK = 128
LANES = 128
ADAPTER_SCALE = 2.0
ROW_GROUP = 8
EXP_SCALE = HEAD ** (-0.5) * math.log2(math.e)

HBM = pl.BlockSpec(memory_space=pl.ANY)
SMEM = pl.BlockSpec(memory_space=pltpu.SMEM)
VMEM = pl.BlockSpec(memory_space=pltpu.VMEM)


def dot_t(a, b):
    return lax.dot_general(a, b, (((1,), (1,)), ((), ())), preferred_element_type=jnp.float32)


def pack_kernel(
    groups, size, positions, ids_ref, fill_ref, len_ref, down_ref, up_ref, live_out, bias_out, *rest,
):
    out_refs, (ids, fill, lengths, window, small_sem, down_sem, up_sem) = rest[:-7], rest[-7:]
    serve = lax.axis_index("serve")
    rows = bias_out.shape[0]
    small = [
        pltpu.make_async_copy(source, target, small_sem.at[k])
        for k, (source, target) in enumerate(((ids_ref, ids), (fill_ref, fill), (len_ref, lengths)))
    ]
    for copy in small:
        copy.start()
    small[0].wait()
    first = serve // size if groups == 2 else 0
    width = down_ref.shape[2]
    cols = up_ref.shape[1]
    copies = []
    starts = []
    for k in range(groups):
        adapter = ids[lax.rem(first + groups - 1 + k, groups)]
        out = out_refs[k] if groups == 2 else out_refs[0].at[(groups - 1 + k) % groups]
        down = pltpu.make_async_copy(
            down_ref.at[0, pl.ds(pl.multiple_of(adapter * RANK, RANK), RANK), :],
            out.at[:, pl.ds(0, width)],
            down_sem.at[k],
        )
        lane = adapter * RANK // LANES * LANES
        up = pltpu.make_async_copy(
            up_ref.at[0, :, pl.ds(pl.multiple_of(lane, LANES), LANES)], window.at[k], up_sem.at[k]
        )
        up.start()
        down.start()
        copies.append((down, up, out))
        starts.append(adapter * RANK - lane)
    small[1].wait()
    small[2].wait()
    total = live_out.shape[0]
    row = lax.broadcasted_iota(jnp.int32, (total, LANES), 0) % rows + lax.rem(serve, size) * rows
    live_out[...] = (row < fill[serve // size]).astype(jnp.float32)
    wide = bias_out.shape[1]
    lanes = lax.broadcasted_iota(jnp.int32, (ROW_GROUP, wide), 1)
    subs = lax.broadcasted_iota(jnp.int32, (ROW_GROUP, wide), 0)
    start = subs * positions
    for at in range(0, rows, ROW_GROUP):
        used = jnp.zeros((ROW_GROUP, wide), jnp.int32)
        for r in range(ROW_GROUP):
            used = jnp.where(subs == r, lengths[at + r], used)
        bias_out[at : at + ROW_GROUP, :] = jnp.where((lanes >= start) & (lanes < start + used), 0.0, -jnp.inf)
    ranks = lax.broadcasted_iota(jnp.int32, (RANK, LANES), 0)
    lanes = lax.broadcasted_iota(jnp.int32, (RANK, LANES), 1)
    for k in range(groups):
        down, up, out = copies[k]
        up.wait()
        chosen = (lanes == ranks + starts[k]).astype(jnp.bfloat16)
        picked = dot_t(chosen, window[k])
        out[:, width : width + LANES] = jnp.concatenate([picked] * (LANES // cols), axis=1).astype(jnp.bfloat16)
    for down, _, _ in copies:
        down.wait()


def pack(block_adapter, block_fill, cache_len, down_store, up_store, query, kv_cache, groups, size):
    width = down_store.shape[2] + LANES
    cols = up_store.shape[1]
    steps, rows, _ = query.shape
    if groups == 2:
        messages = [jax.ShapeDtypeStruct((RANK, width), jnp.bfloat16)] * 2
    else:
        messages = [jax.ShapeDtypeStruct((groups, RANK, width), jnp.bfloat16)]
    operands = (block_adapter, block_fill, cache_len, down_store, up_store)
    return pl.pallas_call(
        functools.partial(pack_kernel, groups, size, kv_cache.shape[1]),
        out_shape=[
            jax.ShapeDtypeStruct((steps * rows, LANES), jnp.float32),
            jax.ShapeDtypeStruct((rows, ROW_GROUP * kv_cache.shape[1]), jnp.float32),
            *messages,
        ],
        in_specs=[HBM] * len(operands),
        out_specs=[VMEM] * (2 + len(messages)),
        scratch_shapes=[
            pltpu.SMEM(block_adapter.shape, jnp.int32),
            pltpu.SMEM(block_fill.shape, jnp.int32),
            pltpu.SMEM(cache_len.shape, jnp.int32),
            pltpu.VMEM((groups, cols, LANES), jnp.bfloat16),
            pltpu.SemaphoreType.DMA((3,)),
            pltpu.SemaphoreType.DMA((groups,)),
            pltpu.SemaphoreType.DMA((groups,)),
        ],
        compiler_params=pltpu.CompilerParams(vmem_limit_bytes=4 << 20),
        name="pack",
    )(*(pltpu.with_memory_space_constraint(x, pltpu.HBM) for x in operands))


def base_kernel(hidden_ref, weight_ref, base_ref):
    steps, rows, width = hidden_ref.shape

    @pl.when(pl.program_id(0) == 0)
    def _():
        base_ref[...] = jnp.zeros_like(base_ref)

    states = hidden_ref[...].reshape(steps * rows, width)
    base_ref[...] += jnp.dot(states, weight_ref[...], preferred_element_type=jnp.float32)


def base_projection(hidden, kv_weight):
    steps, rows, width = hidden.shape
    cols = kv_weight.shape[1]
    chunk = 1024
    return pl.pallas_call(
        base_kernel,
        grid=(width // chunk,),
        out_shape=jax.ShapeDtypeStruct((steps * rows, cols), jnp.float32),
        in_specs=[
            pl.BlockSpec((steps, rows, chunk), lambda i: (0, 0, i)),
            pl.BlockSpec((chunk, cols), lambda i: (i, 0)),
        ],
        out_specs=pl.BlockSpec((steps * rows, cols), lambda i: (0, 0)),
        cost_estimate=pl.CostEstimate(
            flops=2 * steps * rows * width * cols,
            bytes_accessed=2 * width * cols + 2 * steps * rows * width,
            transcendentals=0,
        ),
        compiler_params=pltpu.CompilerParams(vmem_limit_bytes=12 << 20),
        name="base",
    )(hidden, kv_weight)


def cache_kernel(bias_ref, query_hbm, cache_hbm, mix_ref, sum_ref, max_ref, query_ref, cache_ref, query_sem, cache_sem):
    pairs = cache_sem.shape[0]
    brought = 2 * ROW_GROUP
    query_copy = pltpu.make_async_copy(query_hbm, query_ref, query_sem)
    query_copy.start()
    for p in range(pairs):
        at = pl.ds(p * brought, brought)
        pltpu.make_async_copy(cache_hbm.at[at], cache_ref.at[at], cache_sem.at[p]).start()
    query_copy.wait()
    steps, rows, _ = query_ref.shape
    positions = cache_ref.shape[1]
    kv_heads = cache_ref.shape[2] // (2 * HEAD)
    share = query_ref.shape[2] // (kv_heads * HEAD)
    wide = ROW_GROUP * positions
    ones = jnp.ones((wide, HEAD), jnp.bfloat16)

    def pair(p, carry):
        first = pl.multiple_of(p * 2 * ROW_GROUP, 2 * ROW_GROUP)
        at = pl.ds(first, brought)
        pltpu.make_async_copy(cache_hbm.at[at], cache_ref.at[at], cache_sem.at[p]).wait()
        for half in range(2):
            own = pl.ds(pl.multiple_of(first + half * ROW_GROUP, ROW_GROUP), ROW_GROUP)
            bias = bias_ref[own, :]
            for g in range(kv_heads):
                stored = cache_ref[own, :, g * 2 * HEAD : (g + 1) * 2 * HEAD].reshape(wide, 2 * HEAD)
                parts = []
                for s in range(steps):
                    for j in range(share):
                        at = (g * share + j) * HEAD
                        both = query_ref[s, pl.ds(first, 2 * ROW_GROUP), at : at + HEAD]
                        both = both.astype(jnp.float32)
                        parts.append(both[half * ROW_GROUP : (half + 1) * ROW_GROUP])
                stacked = jnp.concatenate(parts, axis=0).astype(jnp.bfloat16)
                scores = dot_t(stacked, stored[:, :HEAD]).reshape(steps * share, ROW_GROUP, wide)
                scores = scores + bias[None]
                highest = jnp.max(scores, axis=-1, keepdims=True)
                weights = jnp.exp2((scores - highest) * EXP_SCALE).reshape(-1, wide).astype(jnp.bfloat16)
                values = jnp.concatenate([stored[:, HEAD:], ones], axis=1)
                mixed = jnp.dot(weights, values, preferred_element_type=jnp.float32)
                mixed = mixed.reshape(steps, share, ROW_GROUP, 2 * HEAD)
                mix_ref[g, :, :, own, :] = mixed[..., :HEAD]
                sum_ref[g, :, :, own, :] = mixed[..., HEAD:]
                max_ref[g, :, :, own, :] = jnp.broadcast_to(
                    highest.reshape(steps, share, ROW_GROUP, 1), (steps, share, ROW_GROUP, HEAD)
                )
        return carry

    lax.fori_loop(0, rows // (2 * ROW_GROUP), pair, 0)


def cache_attention(bias, query, kv_cache):
    steps, rows, heads_width = query.shape
    kv_heads = kv_cache.shape[2] // (2 * HEAD)
    share = heads_width // (kv_heads * HEAD)
    shape = jax.ShapeDtypeStruct((kv_heads, steps, share, rows, HEAD), jnp.float32)
    return pl.pallas_call(
        cache_kernel,
        out_shape=[shape] * 3,
        in_specs=[VMEM, HBM, HBM],
        out_specs=[VMEM] * 3,
        scratch_shapes=[
            pltpu.VMEM(query.shape, query.dtype),
            pltpu.VMEM(kv_cache.shape, kv_cache.dtype),
            pltpu.SemaphoreType.DMA,
            pltpu.SemaphoreType.DMA((rows // (2 * ROW_GROUP),)),
        ],
        cost_estimate=pl.CostEstimate(
            flops=2 * 2 * steps * heads_width * rows * ROW_GROUP * kv_cache.shape[1],
            bytes_accessed=2 * kv_cache.size,
            transcendentals=0,
        ),
        compiler_params=pltpu.CompilerParams(vmem_limit_bytes=12 << 20),
        name="cached",
    )(bias, *(pltpu.with_memory_space_constraint(x, pltpu.HBM) for x in (query, kv_cache)))


def shrink_kernel(groups, size, live_ref, hidden_ref, own_ref, *rest):
    peer_refs, (low_ref, up_ref) = rest[:-2], rest[-2:]
    steps, rows, _ = hidden_ref.shape
    width = own_ref.shape[2] - LANES
    me = lax.axis_index("serve")
    block = me // size
    mine = lax.rem(me, size)
    first = block if groups == 2 else 0
    total = jnp.zeros((steps * rows, RANK), jnp.float32)
    for d, ref in enumerate((own_ref,) + tuple(peer_refs)):
        for e in range(groups):
            source = lax.rem(first + e, groups) * size + (mine ^ d)
            states = hidden_ref[:, :, pl.ds(pl.multiple_of(source * width, LANES), width)]
            factors = ref[e]
            total += dot_t(states.reshape(steps * rows, width), factors[:, :width])
            up_ref[source] = factors[:, width:]
    low_ref[...] = (live_ref[:, :RANK] * total).astype(jnp.bfloat16)


def shrink(live, hidden, parts, groups, size):
    steps, rows, _ = hidden.shape
    return pl.pallas_call(
        functools.partial(shrink_kernel, groups, size),
        out_shape=[
            jax.ShapeDtypeStruct((steps * rows, RANK), jnp.bfloat16),
            jax.ShapeDtypeStruct((groups * size, RANK, LANES), jnp.bfloat16),
        ],
        in_specs=[VMEM] * (2 + len(parts)),
        out_specs=[VMEM] * 2,
        compiler_params=pltpu.CompilerParams(vmem_limit_bytes=4 << 20),
        name="shrink",
    )(live, hidden, *parts)


def final_kernel(
    cols, live_ref, low_ref, other_ref, up_ref, base_ref, query_ref, mix_ref, sum_ref, max_ref,
    new_ref, attn_ref,
):
    steps, rows, _ = query_ref.shape
    kv_heads, _, share = mix_ref.shape[:3]
    total = steps * rows
    live = live_ref[...]
    core = lax.axis_index("tensor")
    keys_low = jnp.where(core == 0, low_ref[...], other_ref[...])
    values_low = jnp.where(core == 0, other_ref[...], low_ref[...])
    lane = lax.broadcasted_iota(jnp.int32, (RANK, LANES), 1)
    each = LANES // cols
    query_row = lax.broadcasted_iota(jnp.int32, (total, total), 0)
    key_row = lax.broadcasted_iota(jnp.int32, (total, total), 1)
    seen = (query_row % rows == key_row % rows) & (key_row // rows <= query_row // rows)
    bias = jnp.where(seen, 0.0, -jnp.inf).reshape(steps, 1, rows, total)
    ones = jnp.ones((total, HEAD), jnp.bfloat16)
    live_row = live[:rows]
    for g in range(kv_heads):
        fresh = []
        for kind, low in enumerate((keys_low, values_low)):
            tile = g * 2 + kind
            up = up_ref[tile * each]
            for k in range(1, each):
                up = jnp.where(lane // cols == k, up_ref[tile * each + k], up)
            delta = jnp.dot(low, up, preferred_element_type=jnp.float32)
            at = slice(tile * HEAD, (tile + 1) * HEAD)
            value = (live * (base_ref[:, at] + ADAPTER_SCALE * delta)).astype(jnp.bfloat16)
            new_ref[:, :, at] = value.reshape(steps, rows, HEAD)
            fresh.append(value)
        for s in range(steps):
            queries = jnp.concatenate(
                [query_ref[s, :, (g * share + j) * HEAD : (g * share + j + 1) * HEAD] for j in range(share)],
                axis=0,
            )
            scores = dot_t(queries, fresh[0]).reshape(share, rows, total) + bias[s]
            cached_max = max_ref[g, s]
            highest = jnp.maximum(cached_max, jnp.max(scores, axis=-1, keepdims=True))
            weights = jnp.exp2((scores - highest[:, :, :total]) * EXP_SCALE)
            keep = jnp.exp2((cached_max - highest) * EXP_SCALE)
            values = jnp.concatenate([fresh[1], ones], axis=1)
            mixed = jnp.dot(
                weights.reshape(-1, total).astype(jnp.bfloat16), values, preferred_element_type=jnp.float32
            ).reshape(share, rows, 2 * HEAD)
            top = mix_ref[g, s] * keep + mixed[..., :HEAD]
            bottom = sum_ref[g, s] * keep + mixed[..., HEAD:]
            result = (top / bottom * live_row[None]).astype(jnp.bfloat16)
            for j in range(share):
                attn_ref[s, :, (g * share + j) * HEAD : (g * share + j + 1) * HEAD] = result[j]


def finish(live, low, other, up, base, query, cached, cols):
    steps, rows, _ = query.shape
    return pl.pallas_call(
        functools.partial(final_kernel, cols),
        out_shape=[
            jax.ShapeDtypeStruct((steps, rows, base.shape[1]), jnp.bfloat16),
            jax.ShapeDtypeStruct(query.shape, jnp.bfloat16),
        ],
        in_specs=[VMEM] * 9,
        out_specs=[VMEM] * 2,
        compiler_params=pltpu.CompilerParams(vmem_limit_bytes=8 << 20),
        name="finish",
    )(live, low, other, up, base, query, *cached)


def local(
    hidden, query, kv_weight, down_store, up_store, kv_cache, cache_len, block_adapter, block_fill
):
    serve = lax.axis_size("serve")
    rows = hidden.shape[1]
    size = BLK // rows
    groups = serve // size
    live, bias, *packed = pack(
        block_adapter, block_fill, cache_len, down_store, up_store, query, kv_cache, groups, size
    )
    if groups == 2:
        other, own = packed
        swap = [(i, (i + size) % serve) for i in range(serve)]
        arrived = jnp.stack([own, lax.ppermute(other, "serve", swap)])
    else:
        same = [[g * size + j for g in range(groups)] for j in range(size)]
        arrived = lax.all_to_all(packed[0], "serve", 0, 0, axis_index_groups=same, tiled=True)
    cached = cache_attention(bias, query, kv_cache)
    arrived, cached, hidden = lax.optimization_barrier((arrived, cached, hidden))
    parts = [arrived]
    for d in range(1, size):
        parts.append(lax.ppermute(arrived, "serve", [(i, i ^ d) for i in range(serve)]))
    base = base_projection(hidden, kv_weight)
    parts, base = lax.optimization_barrier((parts, base))
    low, up = shrink(live, hidden, parts, groups, size)
    other_low = lax.ppermute(low, "tensor", [(0, 1), (1, 0)])
    return tuple(finish(live, low, other_low, up, base, query, cached, up_store.shape[1]))


def solution(mesh):
    in_specs = (
        P(None, ("parts", "serve"), None),
        P(None, ("parts", "serve"), "tensor"),
        P(None, "tensor"),
        P("tensor", None, "serve"),
        P("tensor", "serve", None),
        P(("parts", "serve"), None, "tensor"),
        P(("parts", "serve")),
        P("parts"),
        P("parts"),
    )
    out_specs = (P(None, ("parts", "serve"), "tensor"), P(None, ("parts", "serve"), "tensor"))
    return jax.shard_map(local, mesh=mesh, in_specs=in_specs, out_specs=out_specs, check_vma=False)
```

```python
import functools
import math

import jax
import jax.numpy as jnp
from jax import lax
from jax.experimental import pallas as pl
from jax.experimental.pallas import tpu as pltpu
from jax.sharding import PartitionSpec as P

HEAD = 128
RANK = 16
BLK = 128
LANES = 128
ADAPTER_SCALE = 2.0
ROW_GROUP = 8
EXP_SCALE = HEAD ** (-0.5) * math.log2(math.e)

HBM = pl.BlockSpec(memory_space=pl.ANY)
SMEM = pl.BlockSpec(memory_space=pltpu.SMEM)
VMEM = pl.BlockSpec(memory_space=pltpu.VMEM)


def dot_t(a, b):
    return lax.dot_general(a, b, (((1,), (1,)), ((), ())), preferred_element_type=jnp.float32)


def pack_kernel(
    groups, size, positions, ids_ref, fill_ref, len_ref, down_ref, up_ref, live_out, bias_out, *rest,
):
    out_refs, (ids, fill, lengths, window, small_sem, down_sem, up_sem) = rest[:-7], rest[-7:]
    serve = lax.axis_index("serve")
    rows = bias_out.shape[0]
    small = [
        pltpu.make_async_copy(source, target, small_sem.at[k])
        for k, (source, target) in enumerate(((ids_ref, ids), (fill_ref, fill), (len_ref, lengths)))
    ]
    for copy in small:
        copy.start()
    small[0].wait()
    first = serve // size if groups == 2 else 0
    width = down_ref.shape[2]
    cols = up_ref.shape[1]
    copies = []
    starts = []
    for k in range(groups):
        adapter = ids[lax.rem(first + groups - 1 + k, groups)]
        out = out_refs[k] if groups == 2 else out_refs[0].at[(groups - 1 + k) % groups]
        down = pltpu.make_async_copy(
            down_ref.at[0, pl.ds(pl.multiple_of(adapter * RANK, RANK), RANK), :],
            out.at[:, pl.ds(0, width)],
            down_sem.at[k],
        )
        lane = adapter * RANK // LANES * LANES
        up = pltpu.make_async_copy(
            up_ref.at[0, :, pl.ds(pl.multiple_of(lane, LANES), LANES)], window.at[k], up_sem.at[k]
        )
        up.start()
        down.start()
        copies.append((down, up, out))
        starts.append(adapter * RANK - lane)
    small[1].wait()
    small[2].wait()
    total = live_out.shape[0]
    row = lax.broadcasted_iota(jnp.int32, (total, LANES), 0) % rows + lax.rem(serve, size) * rows
    live_out[...] = (row < fill[serve // size]).astype(jnp.float32)
    wide = bias_out.shape[1]
    lanes = lax.broadcasted_iota(jnp.int32, (ROW_GROUP, wide), 1)
    subs = lax.broadcasted_iota(jnp.int32, (ROW_GROUP, wide), 0)
    start = subs * positions
    for at in range(0, rows, ROW_GROUP):
        used = jnp.zeros((ROW_GROUP, wide), jnp.int32)
        for r in range(ROW_GROUP):
            used = jnp.where(subs == r, lengths[at + r], used)
        bias_out[at : at + ROW_GROUP, :] = jnp.where((lanes >= start) & (lanes < start + used), 0.0, -jnp.inf)
    ranks = lax.broadcasted_iota(jnp.int32, (RANK, LANES), 0)
    lanes = lax.broadcasted_iota(jnp.int32, (RANK, LANES), 1)
    for k in range(groups):
        down, up, out = copies[k]
        up.wait()
        chosen = (lanes == ranks + starts[k]).astype(jnp.bfloat16)
        picked = dot_t(chosen, window[k])
        out[:, width : width + LANES] = jnp.concatenate([picked] * (LANES // cols), axis=1).astype(jnp.bfloat16)
    for down, _, _ in copies:
        down.wait()


def pack(block_adapter, block_fill, cache_len, down_store, up_store, query, kv_cache, groups, size):
    width = down_store.shape[2] + LANES
    cols = up_store.shape[1]
    steps, rows, _ = query.shape
    if groups == 2:
        messages = [jax.ShapeDtypeStruct((RANK, width), jnp.bfloat16)] * 2
    else:
        messages = [jax.ShapeDtypeStruct((groups, RANK, width), jnp.bfloat16)]
    operands = (block_adapter, block_fill, cache_len, down_store, up_store)
    return pl.pallas_call(
        functools.partial(pack_kernel, groups, size, kv_cache.shape[1]),
        out_shape=[
            jax.ShapeDtypeStruct((steps * rows, LANES), jnp.float32),
            jax.ShapeDtypeStruct((rows, ROW_GROUP * kv_cache.shape[1]), jnp.float32),
            *messages,
        ],
        in_specs=[HBM] * len(operands),
        out_specs=[VMEM] * (2 + len(messages)),
        scratch_shapes=[
            pltpu.SMEM(block_adapter.shape, jnp.int32),
            pltpu.SMEM(block_fill.shape, jnp.int32),
            pltpu.SMEM(cache_len.shape, jnp.int32),
            pltpu.VMEM((groups, cols, LANES), jnp.bfloat16),
            pltpu.SemaphoreType.DMA((3,)),
            pltpu.SemaphoreType.DMA((groups,)),
            pltpu.SemaphoreType.DMA((groups,)),
        ],
        compiler_params=pltpu.CompilerParams(vmem_limit_bytes=4 << 20),
        name="pack",
    )(*(pltpu.with_memory_space_constraint(x, pltpu.HBM) for x in operands))


def base_kernel(hidden_ref, weight_ref, base_ref):
    steps, rows, width = hidden_ref.shape

    @pl.when(pl.program_id(0) == 0)
    def _():
        base_ref[...] = jnp.zeros_like(base_ref)

    states = hidden_ref[...].reshape(steps * rows, width)
    base_ref[...] += jnp.dot(states, weight_ref[...], preferred_element_type=jnp.float32)


def base_projection(hidden, kv_weight):
    steps, rows, width = hidden.shape
    cols = kv_weight.shape[1]
    chunk = 1024
    return pl.pallas_call(
        base_kernel,
        grid=(width // chunk,),
        out_shape=jax.ShapeDtypeStruct((steps * rows, cols), jnp.float32),
        in_specs=[
            pl.BlockSpec((steps, rows, chunk), lambda i: (0, 0, i)),
            pl.BlockSpec((chunk, cols), lambda i: (i, 0)),
        ],
        out_specs=pl.BlockSpec((steps * rows, cols), lambda i: (0, 0)),
        cost_estimate=pl.CostEstimate(
            flops=2 * steps * rows * width * cols,
            bytes_accessed=2 * width * cols + 2 * steps * rows * width,
            transcendentals=0,
        ),
        compiler_params=pltpu.CompilerParams(vmem_limit_bytes=12 << 20),
        name="base",
    )(hidden, kv_weight)


def cache_kernel(bias_ref, query_ref, cache_ref, mix_ref, sum_ref, max_ref):
    steps, rows, _ = query_ref.shape
    positions = cache_ref.shape[1]
    kv_heads = cache_ref.shape[2] // (2 * HEAD)
    share = query_ref.shape[2] // (kv_heads * HEAD)
    wide = ROW_GROUP * positions
    ones = jnp.ones((wide, HEAD), jnp.bfloat16)

    def pair(p, carry):
        first = pl.multiple_of(p * 2 * ROW_GROUP, 2 * ROW_GROUP)
        for half in range(2):
            own = pl.ds(pl.multiple_of(first + half * ROW_GROUP, ROW_GROUP), ROW_GROUP)
            bias = bias_ref[own, :]
            for g in range(kv_heads):
                stored = cache_ref[own, :, g * 2 * HEAD : (g + 1) * 2 * HEAD].reshape(wide, 2 * HEAD)
                parts = []
                for s in range(steps):
                    for j in range(share):
                        at = (g * share + j) * HEAD
                        both = query_ref[s, pl.ds(first, 2 * ROW_GROUP), at : at + HEAD]
                        both = both.astype(jnp.float32)
                        parts.append(both[half * ROW_GROUP : (half + 1) * ROW_GROUP])
                stacked = jnp.concatenate(parts, axis=0).astype(jnp.bfloat16)
                scores = dot_t(stacked, stored[:, :HEAD]).reshape(steps * share, ROW_GROUP, wide)
                scores = scores + bias[None]
                highest = jnp.max(scores, axis=-1, keepdims=True)
                weights = jnp.exp2((scores - highest) * EXP_SCALE).reshape(-1, wide).astype(jnp.bfloat16)
                values = jnp.concatenate([stored[:, HEAD:], ones], axis=1)
                mixed = jnp.dot(weights, values, preferred_element_type=jnp.float32)
                mixed = mixed.reshape(steps, share, ROW_GROUP, 2 * HEAD)
                mix_ref[g, :, :, own, :] = mixed[..., :HEAD]
                sum_ref[g, :, :, own, :] = mixed[..., HEAD:]
                max_ref[g, :, :, own, :] = jnp.broadcast_to(
                    highest.reshape(steps, share, ROW_GROUP, 1), (steps, share, ROW_GROUP, HEAD)
                )
        return carry

    lax.fori_loop(0, rows // (2 * ROW_GROUP), pair, 0)


def cache_attention(bias, query, kv_cache):
    steps, rows, heads_width = query.shape
    kv_heads = kv_cache.shape[2] // (2 * HEAD)
    share = heads_width // (kv_heads * HEAD)
    shape = jax.ShapeDtypeStruct((kv_heads, steps, share, rows, HEAD), jnp.float32)
    return pl.pallas_call(
        cache_kernel,
        out_shape=[shape] * 3,
        in_specs=[VMEM] * 3,
        out_specs=[VMEM] * 3,
        cost_estimate=pl.CostEstimate(
            flops=40 * 2 * 2 * steps * heads_width * rows * ROW_GROUP * kv_cache.shape[1],
            bytes_accessed=2 * kv_cache.size,
            transcendentals=0,
        ),
        compiler_params=pltpu.CompilerParams(vmem_limit_bytes=12 << 20),
        name="cached",
    )(bias, query, kv_cache)


def pieces(groups, size):
    return [(e, d, ((groups == 2 and e == 1) != (d > 0))) for d in range(size) for e in range(groups)]


def piece_source(groups, size, e, d):
    me = lax.axis_index("serve")
    first = me // size if groups == 2 else 0
    return lax.rem(first + e, groups) * size + (lax.rem(me, size) ^ d)


def shrink_kernel(groups, size, hidden_ref, *rest):
    part_refs, (send_ref, up_ref) = rest[:-2], rest[-2:]
    steps, rows, _ = hidden_ref.shape
    total = steps * rows
    width = part_refs[0].shape[2] - LANES
    sums = [jnp.zeros((total, RANK), jnp.float32)] * 2
    at = 2 * total
    for e, d, crossed in pieces(groups, size):
        source = piece_source(groups, size, e, d)
        states = hidden_ref[:, :, pl.ds(pl.multiple_of(source * width, LANES), width)]
        factors = part_refs[d][e]
        sums[crossed] = sums[crossed] + dot_t(states.reshape(total, width), factors[:, :width])
        if crossed:
            send_ref[at : at + RANK, :] = factors[:, width:].astype(jnp.float32)
            at += RANK
        else:
            up_ref[source] = factors[:, width:]
    send_ref[:total, :RANK] = sums[0]
    send_ref[total : 2 * total, :RANK] = sums[1]


def shrink(hidden, parts, groups, size):
    steps, rows, _ = hidden.shape
    crossed = sum(c for _, _, c in pieces(groups, size))
    return pl.pallas_call(
        functools.partial(shrink_kernel, groups, size),
        out_shape=[
            jax.ShapeDtypeStruct((2 * steps * rows + crossed * RANK, LANES), jnp.float32),
            jax.ShapeDtypeStruct((groups * size, RANK, LANES), jnp.bfloat16),
        ],
        in_specs=[VMEM] * (1 + len(parts)),
        out_specs=[VMEM] * 2,
        compiler_params=pltpu.CompilerParams(vmem_limit_bytes=4 << 20),
        name="shrink",
    )(hidden, *parts)


def final_kernel(
    groups, size, cols, live_ref, sent_ref, came_ref, straight_ref, base_ref, query_ref, mix_ref, sum_ref, max_ref,
    new_ref, attn_ref, up_ref,
):
    steps, rows, _ = query_ref.shape
    kv_heads, _, share = mix_ref.shape[:3]
    total = steps * rows
    live = live_ref[...]
    core = lax.axis_index("tensor")
    own_sum = sent_ref[:total, :RANK] + came_ref[total : 2 * total, :RANK]
    other_sum = sent_ref[total : 2 * total, :RANK] + came_ref[:total, :RANK]
    keys_low = (live[:, :RANK] * jnp.where(core == 0, own_sum, other_sum)).astype(jnp.bfloat16)
    values_low = (live[:, :RANK] * jnp.where(core == 0, other_sum, own_sum)).astype(jnp.bfloat16)
    at = 2 * total
    for e, d, crossed in pieces(groups, size):
        source = piece_source(groups, size, e, d)
        if crossed:
            up_ref[source] = came_ref[at : at + RANK, :].astype(jnp.bfloat16)
            at += RANK
        else:
            up_ref[source] = straight_ref[source]
    lane = lax.broadcasted_iota(jnp.int32, (RANK, LANES), 1)
    each = LANES // cols
    query_row = lax.broadcasted_iota(jnp.int32, (total, total), 0)
    key_row = lax.broadcasted_iota(jnp.int32, (total, total), 1)
    seen = (query_row % rows == key_row % rows) & (key_row // rows <= query_row // rows)
    bias = jnp.where(seen, 0.0, -jnp.inf).reshape(steps, 1, rows, total)
    ones = jnp.ones((total, HEAD), jnp.bfloat16)
    live_row = live[:rows]
    fresh = []
    for tile in range(2 * kv_heads):
        up = up_ref[tile * each]
        for k in range(1, each):
            up = jnp.where(lane // cols == k, up_ref[tile * each + k], up)
        low = keys_low if tile % 2 == 0 else values_low
        delta = jnp.dot(low, up, preferred_element_type=jnp.float32)
        at = slice(tile * HEAD, (tile + 1) * HEAD)
        value = (live * (base_ref[:, at] + ADAPTER_SCALE * delta)).astype(jnp.bfloat16)
        new_ref[:, :, at] = value.reshape(steps, rows, HEAD)
        fresh.append(value)
    todo = [(g, s) for g in range(kv_heads) for s in range(steps)]
    found = []
    for g, s in todo:
        queries = jnp.concatenate(
            [query_ref[s, :, (g * share + j) * HEAD : (g * share + j + 1) * HEAD] for j in range(share)], axis=0
        )
        scores = dot_t(queries, fresh[2 * g]).reshape(share, rows, total) + bias[s]
        found.append((scores, jnp.max(scores, axis=-1, keepdims=True)))
    for (g, s), (scores, most) in zip(todo, found):
        cached_max = max_ref[g, s]
        highest = jnp.maximum(cached_max, most)
        weights = jnp.exp2((scores - highest[:, :, :total]) * EXP_SCALE)
        keep = jnp.exp2((cached_max - highest) * EXP_SCALE)
        values = jnp.concatenate([fresh[2 * g + 1], ones], axis=1)
        mixed = jnp.dot(
            weights.reshape(-1, total).astype(jnp.bfloat16), values, preferred_element_type=jnp.float32
        ).reshape(share, rows, 2 * HEAD)
        top = mix_ref[g, s] * keep + mixed[..., :HEAD]
        bottom = sum_ref[g, s] * keep + mixed[..., HEAD:]
        result = (top / bottom * live_row[None]).astype(jnp.bfloat16)
        for j in range(share):
            attn_ref[s, :, (g * share + j) * HEAD : (g * share + j + 1) * HEAD] = result[j]


def finish(live, sent, came, up, base, query, cached, groups, size, cols):
    steps, rows, _ = query.shape
    return pl.pallas_call(
        functools.partial(final_kernel, groups, size, cols),
        out_shape=[
            jax.ShapeDtypeStruct((steps, rows, base.shape[1]), jnp.bfloat16),
            jax.ShapeDtypeStruct(query.shape, jnp.bfloat16),
        ],
        in_specs=[VMEM] * 9,
        out_specs=[VMEM] * 2,
        scratch_shapes=[pltpu.VMEM(up.shape, up.dtype)],
        compiler_params=pltpu.CompilerParams(vmem_limit_bytes=8 << 20),
        name="finish",
    )(live, sent, came, up, base, query, *cached)


def local(
    hidden, query, kv_weight, down_store, up_store, kv_cache, cache_len, block_adapter, block_fill
):
    serve = lax.axis_size("serve")
    rows = hidden.shape[1]
    size = BLK // rows
    groups = serve // size
    both = ("serve", "tensor")

    def crossing(d):
        return [(i * 2 + t, (i ^ d) * 2 + 1 - t) for i in range(serve) for t in range(2)]

    live, bias, *packed = pack(
        block_adapter, block_fill, cache_len, down_store, up_store, query, kv_cache, groups, size
    )
    if groups == 2:
        other, own = packed
        arrived = jnp.stack([own, lax.ppermute(other, both, crossing(size))])
    else:
        same = [[g * size + j for g in range(groups)] for j in range(size)]
        arrived = lax.all_to_all(packed[0], "serve", 0, 0, axis_index_groups=same, tiled=True)
    cached = cache_attention(bias, query, kv_cache)
    arrived, cached, hidden = lax.optimization_barrier((arrived, cached, hidden))
    parts = [arrived]
    for d in range(1, size):
        parts.append(lax.ppermute(arrived, both, crossing(d)))
    base = base_projection(hidden, kv_weight)
    parts, base = lax.optimization_barrier((parts, base))
    sent, up = shrink(hidden, parts, groups, size)
    came = lax.ppermute(sent, "tensor", [(0, 1), (1, 0)])
    return tuple(finish(live, sent, came, up, base, query, cached, groups, size, up_store.shape[1]))


def solution(mesh):
    in_specs = (
        P(None, ("parts", "serve"), None),
        P(None, ("parts", "serve"), "tensor"),
        P(None, "tensor"),
        P("tensor", None, "serve"),
        P("tensor", "serve", None),
        P(("parts", "serve"), None, "tensor"),
        P(("parts", "serve")),
        P("parts"),
        P("parts"),
    )
    out_specs = (P(None, ("parts", "serve"), "tensor"), P(None, ("parts", "serve"), "tensor"))
    return jax.shard_map(local, mesh=mesh, in_specs=in_specs, out_specs=out_specs, check_vma=False)
```

```python
import functools
import math

import jax
import jax.numpy as jnp
from jax import lax
from jax.experimental import pallas as pl
from jax.experimental.pallas import tpu as pltpu
from jax.sharding import PartitionSpec as P

HEAD = 128
RANK = 16
BLK = 128
LANES = 128
ADAPTER_SCALE = 2.0
ROW_GROUP = 8
CHUNK = 1024
HEAD_CHUNKS = 3
EXP_SCALE = HEAD ** (-0.5) * math.log2(math.e)

HBM = pl.BlockSpec(memory_space=pl.ANY)
SMEM = pl.BlockSpec(memory_space=pltpu.SMEM)
VMEM = pl.BlockSpec(memory_space=pltpu.VMEM)


def dot_t(a, b):
    return lax.dot_general(a, b, (((1,), (1,)), ((), ())), preferred_element_type=jnp.float32)


def pack_kernel(
    groups, size, positions, ids_ref, fill_ref, len_ref, down_ref, up_ref, live_out, bias_out, *rest,
):
    out_refs, (ids, fill, lengths, window, small_sem, down_sem, up_sem) = rest[:-7], rest[-7:]
    serve = lax.axis_index("serve")
    rows = bias_out.shape[0]
    small = [
        pltpu.make_async_copy(source, target, small_sem.at[k])
        for k, (source, target) in enumerate(((ids_ref, ids), (fill_ref, fill), (len_ref, lengths)))
    ]
    for copy in small:
        copy.start()
    small[0].wait()
    first = serve // size if groups == 2 else 0
    width = down_ref.shape[2]
    cols = up_ref.shape[1]
    copies = []
    starts = []
    for k in range(groups):
        adapter = ids[lax.rem(first + groups - 1 + k, groups)]
        out = out_refs[k] if groups == 2 else out_refs[0].at[(groups - 1 + k) % groups]
        down = pltpu.make_async_copy(
            down_ref.at[0, pl.ds(pl.multiple_of(adapter * RANK, RANK), RANK), :],
            out.at[:, pl.ds(0, width)],
            down_sem.at[k],
        )
        lane = adapter * RANK // LANES * LANES
        up = pltpu.make_async_copy(
            up_ref.at[0, :, pl.ds(pl.multiple_of(lane, LANES), LANES)], window.at[k], up_sem.at[k]
        )
        up.start()
        down.start()
        copies.append((down, up, out))
        starts.append(adapter * RANK - lane)
    small[1].wait()
    small[2].wait()
    total = live_out.shape[0]
    row = lax.broadcasted_iota(jnp.int32, (total, LANES), 0) % rows + lax.rem(serve, size) * rows
    live_out[...] = (row < fill[serve // size]).astype(jnp.float32)
    wide = bias_out.shape[1]
    lanes = lax.broadcasted_iota(jnp.int32, (ROW_GROUP, wide), 1)
    subs = lax.broadcasted_iota(jnp.int32, (ROW_GROUP, wide), 0)
    start = subs * positions
    for at in range(0, rows, ROW_GROUP):
        used = jnp.zeros((ROW_GROUP, wide), jnp.int32)
        for r in range(ROW_GROUP):
            used = jnp.where(subs == r, lengths[at + r], used)
        bias_out[at : at + ROW_GROUP, :] = jnp.where((lanes >= start) & (lanes < start + used), 0.0, -jnp.inf)
    ranks = lax.broadcasted_iota(jnp.int32, (RANK, LANES), 0)
    lanes = lax.broadcasted_iota(jnp.int32, (RANK, LANES), 1)
    chosen = [(lanes == ranks + start).astype(jnp.bfloat16) for start in starts]
    for _, up, _ in copies:
        up.wait()
    picked = [dot_t(chosen[k], jnp.concatenate([window[k]] * (LANES // cols), axis=0)) for k in range(groups)]
    for k in range(groups):
        copies[k][2][:, width : width + LANES] = picked[k].astype(jnp.bfloat16)
    for down, _, _ in copies:
        down.wait()


def pack(block_adapter, block_fill, cache_len, down_store, up_store, query, kv_cache, groups, size):
    width = down_store.shape[2] + LANES
    cols = up_store.shape[1]
    steps, rows, _ = query.shape
    if groups == 2:
        messages = [jax.ShapeDtypeStruct((RANK, width), jnp.bfloat16)] * 2
    else:
        messages = [jax.ShapeDtypeStruct((groups, RANK, width), jnp.bfloat16)]
    operands = (block_adapter, block_fill, cache_len, down_store, up_store)
    return pl.pallas_call(
        functools.partial(pack_kernel, groups, size, kv_cache.shape[1]),
        out_shape=[
            jax.ShapeDtypeStruct((steps * rows, LANES), jnp.float32),
            jax.ShapeDtypeStruct((rows, ROW_GROUP * kv_cache.shape[1]), jnp.float32),
            *messages,
        ],
        in_specs=[HBM] * len(operands),
        out_specs=[VMEM] * (2 + len(messages)),
        scratch_shapes=[
            pltpu.SMEM(block_adapter.shape, jnp.int32),
            pltpu.SMEM(block_fill.shape, jnp.int32),
            pltpu.SMEM(cache_len.shape, jnp.int32),
            pltpu.VMEM((groups, cols, LANES), jnp.bfloat16),
            pltpu.SemaphoreType.DMA((3,)),
            pltpu.SemaphoreType.DMA((groups,)),
            pltpu.SemaphoreType.DMA((groups,)),
        ],
        compiler_params=pltpu.CompilerParams(vmem_limit_bytes=4 << 20),
        name="pack",
    )(*(pltpu.with_memory_space_constraint(x, pltpu.HBM) for x in operands))


def base_kernel(hidden_ref, head_ref, weight_hbm, base_ref, tail_ref, tail_sem):
    steps, rows, _ = hidden_ref.shape
    head = head_ref.shape[0]
    chunks = tail_sem.shape[0]

    def tail(i):
        at = pl.multiple_of(i * CHUNK, CHUNK)
        source = weight_hbm.at[pl.ds(pl.multiple_of(head + i * CHUNK, CHUNK), CHUNK)]
        return pltpu.make_async_copy(source, tail_ref.at[pl.ds(at, CHUNK)], tail_sem.at[i])

    for i in range(chunks):
        tail(i).start()
    states = hidden_ref[:, :, :head].reshape(steps * rows, head)
    base_ref[...] = jnp.dot(states, head_ref[...], preferred_element_type=jnp.float32)

    def step(i, carry):
        tail(i).wait()
        states = hidden_ref[:, :, pl.ds(pl.multiple_of(head + i * CHUNK, CHUNK), CHUNK)]
        part = tail_ref[pl.ds(pl.multiple_of(i * CHUNK, CHUNK), CHUNK), :]
        base_ref[...] += jnp.dot(states.reshape(steps * rows, CHUNK), part, preferred_element_type=jnp.float32)
        return carry

    lax.fori_loop(0, chunks, step, 0)


def base_projection(hidden, head, kv_weight):
    steps, rows, width = hidden.shape
    cols = kv_weight.shape[1]
    chunks = (width - head.shape[0]) // CHUNK
    return pl.pallas_call(
        base_kernel,
        out_shape=jax.ShapeDtypeStruct((steps * rows, cols), jnp.float32),
        in_specs=[VMEM, VMEM, HBM],
        out_specs=VMEM,
        scratch_shapes=[
            pltpu.VMEM((chunks * CHUNK, cols), kv_weight.dtype),
            pltpu.SemaphoreType.DMA((chunks,)),
        ],
        cost_estimate=pl.CostEstimate(
            flops=2 * steps * rows * width * cols,
            bytes_accessed=2 * width * cols + 2 * steps * rows * width,
            transcendentals=0,
        ),
        compiler_params=pltpu.CompilerParams(vmem_limit_bytes=14 << 20),
        name="base",
    )(hidden, head, pltpu.with_memory_space_constraint(kv_weight, pltpu.HBM))


def cache_kernel(bias_ref, query_ref, cache_ref, weight_hbm, mix_ref, sum_ref, max_ref, head_ref, head_sem):
    head_copy = pltpu.make_async_copy(weight_hbm.at[pl.ds(0, head_ref.shape[0])], head_ref, head_sem)
    head_copy.start()
    steps, rows, _ = query_ref.shape
    positions = cache_ref.shape[1]
    kv_heads = cache_ref.shape[2] // (2 * HEAD)
    share = query_ref.shape[2] // (kv_heads * HEAD)
    wide = ROW_GROUP * positions
    ones = jnp.ones((wide, HEAD), jnp.bfloat16)

    def pair(p, carry):
        first = pl.multiple_of(p * 2 * ROW_GROUP, 2 * ROW_GROUP)
        for half in range(2):
            own = pl.ds(pl.multiple_of(first + half * ROW_GROUP, ROW_GROUP), ROW_GROUP)
            bias = bias_ref[own, :]
            for g in range(kv_heads):
                stored = cache_ref[own, :, g * 2 * HEAD : (g + 1) * 2 * HEAD].reshape(wide, 2 * HEAD)
                parts = []
                for s in range(steps):
                    for j in range(share):
                        at = (g * share + j) * HEAD
                        both = query_ref[s, pl.ds(first, 2 * ROW_GROUP), at : at + HEAD]
                        both = both.astype(jnp.float32)
                        parts.append(both[half * ROW_GROUP : (half + 1) * ROW_GROUP])
                stacked = jnp.concatenate(parts, axis=0).astype(jnp.bfloat16)
                scores = dot_t(stacked, stored[:, :HEAD]).reshape(steps * share, ROW_GROUP, wide)
                scores = scores + bias[None]
                highest = jnp.max(scores, axis=-1, keepdims=True)
                weights = jnp.exp2((scores - highest) * EXP_SCALE).reshape(-1, wide).astype(jnp.bfloat16)
                values = jnp.concatenate([stored[:, HEAD:], ones], axis=1)
                mixed = jnp.dot(weights, values, preferred_element_type=jnp.float32)
                mixed = mixed.reshape(steps, share, ROW_GROUP, 2 * HEAD)
                mix_ref[g, :, :, own, :] = mixed[..., :HEAD]
                sum_ref[g, :, :, own, :] = mixed[..., HEAD:]
                max_ref[g, :, :, own, :] = jnp.broadcast_to(
                    highest.reshape(steps, share, ROW_GROUP, 1), (steps, share, ROW_GROUP, HEAD)
                )
        return carry

    lax.fori_loop(0, rows // (2 * ROW_GROUP), pair, 0)
    head_copy.wait()


def cache_attention(bias, query, kv_cache, kv_weight):
    steps, rows, heads_width = query.shape
    kv_heads = kv_cache.shape[2] // (2 * HEAD)
    share = heads_width // (kv_heads * HEAD)
    head = jax.ShapeDtypeStruct((HEAD_CHUNKS * CHUNK, kv_weight.shape[1]), kv_weight.dtype)
    shape = jax.ShapeDtypeStruct((kv_heads, steps, share, rows, HEAD), jnp.float32)
    return pl.pallas_call(
        cache_kernel,
        out_shape=[shape] * 3 + [head],
        in_specs=[VMEM] * 3 + [HBM],
        out_specs=[VMEM] * 4,
        scratch_shapes=[pltpu.SemaphoreType.DMA],
        cost_estimate=pl.CostEstimate(
            flops=40 * 2 * 2 * steps * heads_width * rows * ROW_GROUP * kv_cache.shape[1],
            bytes_accessed=2 * kv_cache.size,
            transcendentals=0,
        ),
        compiler_params=pltpu.CompilerParams(vmem_limit_bytes=12 << 20),
        name="cached",
    )(bias, query, kv_cache, pltpu.with_memory_space_constraint(kv_weight, pltpu.HBM))


def pieces(groups, size):
    return [(e, d, ((groups == 2 and e == 1) != (d > 0))) for d in range(size) for e in range(groups)]


def piece_source(groups, size, e, d):
    me = lax.axis_index("serve")
    first = me // size if groups == 2 else 0
    return lax.rem(first + e, groups) * size + (lax.rem(me, size) ^ d)


def shrink_kernel(groups, size, hidden_ref, *rest):
    part_refs, (send_ref, up_ref) = rest[:-2], rest[-2:]
    steps, rows, _ = hidden_ref.shape
    total = steps * rows
    width = part_refs[0].shape[2] - LANES
    sums = [jnp.zeros((total, RANK), jnp.float32)] * 2
    at = 2 * total
    for e, d, crossed in pieces(groups, size):
        source = piece_source(groups, size, e, d)
        states = hidden_ref[:, :, pl.ds(pl.multiple_of(source * width, LANES), width)]
        factors = part_refs[d][e]
        sums[crossed] = sums[crossed] + dot_t(states.reshape(total, width), factors[:, :width])
        if crossed:
            send_ref[at : at + RANK, :] = factors[:, width:].astype(jnp.float32)
            at += RANK
        else:
            up_ref[source] = factors[:, width:]
    send_ref[:total, :RANK] = sums[0]
    send_ref[total : 2 * total, :RANK] = sums[1]


def shrink(hidden, parts, groups, size):
    steps, rows, _ = hidden.shape
    crossed = sum(c for _, _, c in pieces(groups, size))
    return pl.pallas_call(
        functools.partial(shrink_kernel, groups, size),
        out_shape=[
            jax.ShapeDtypeStruct((2 * steps * rows + crossed * RANK, LANES), jnp.float32),
            jax.ShapeDtypeStruct((groups * size, RANK, LANES), jnp.bfloat16),
        ],
        in_specs=[VMEM] * (1 + len(parts)),
        out_specs=[VMEM] * 2,
        compiler_params=pltpu.CompilerParams(vmem_limit_bytes=4 << 20),
        name="shrink",
    )(hidden, *parts)


def final_kernel(
    groups, size, cols, live_ref, sent_ref, came_ref, straight_ref, base_ref, query_ref, mix_ref, sum_ref, max_ref,
    new_ref, attn_ref, up_ref,
):
    steps, rows, _ = query_ref.shape
    kv_heads, _, share = mix_ref.shape[:3]
    total = steps * rows
    live = live_ref[...]
    core = lax.axis_index("tensor")
    own_sum = sent_ref[:total, :RANK] + came_ref[total : 2 * total, :RANK]
    other_sum = sent_ref[total : 2 * total, :RANK] + came_ref[:total, :RANK]
    keys_low = (live[:, :RANK] * jnp.where(core == 0, own_sum, other_sum)).astype(jnp.bfloat16)
    values_low = (live[:, :RANK] * jnp.where(core == 0, other_sum, own_sum)).astype(jnp.bfloat16)
    at = 2 * total
    for e, d, crossed in pieces(groups, size):
        source = piece_source(groups, size, e, d)
        if crossed:
            up_ref[source] = came_ref[at : at + RANK, :].astype(jnp.bfloat16)
            at += RANK
        else:
            up_ref[source] = straight_ref[source]
    lane = lax.broadcasted_iota(jnp.int32, (RANK, LANES), 1)
    each = LANES // cols
    query_row = lax.broadcasted_iota(jnp.int32, (total, total), 0)
    key_row = lax.broadcasted_iota(jnp.int32, (total, total), 1)
    seen = (query_row % rows == key_row % rows) & (key_row // rows <= query_row // rows)
    bias = jnp.where(seen, 0.0, -jnp.inf).reshape(steps, 1, rows, total)
    ones = jnp.ones((total, HEAD), jnp.bfloat16)
    live_row = live[:rows]
    fresh = []
    for tile in range(2 * kv_heads):
        up = up_ref[tile * each]
        for k in range(1, each):
            up = jnp.where(lane // cols == k, up_ref[tile * each + k], up)
        low = keys_low if tile % 2 == 0 else values_low
        delta = jnp.dot(low, up, preferred_element_type=jnp.float32)
        at = slice(tile * HEAD, (tile + 1) * HEAD)
        value = (live * (base_ref[:, at] + ADAPTER_SCALE * delta)).astype(jnp.bfloat16)
        new_ref[:, :, at] = value.reshape(steps, rows, HEAD)
        fresh.append(value)
    todo = [(g, s) for g in range(kv_heads) for s in range(steps)]
    found = []
    for g, s in todo:
        queries = jnp.concatenate(
            [query_ref[s, :, (g * share + j) * HEAD : (g * share + j + 1) * HEAD] for j in range(share)], axis=0
        )
        scores = dot_t(queries, fresh[2 * g]).reshape(share, rows, total) + bias[s]
        found.append((scores, jnp.max(scores, axis=-1, keepdims=True)))
    for (g, s), (scores, most) in zip(todo, found):
        cached_max = max_ref[g, s]
        highest = jnp.maximum(cached_max, most)
        weights = jnp.exp2((scores - highest[:, :, :total]) * EXP_SCALE)
        keep = jnp.exp2((cached_max - highest) * EXP_SCALE)
        values = jnp.concatenate([fresh[2 * g + 1], ones], axis=1)
        mixed = jnp.dot(
            weights.reshape(-1, total).astype(jnp.bfloat16), values, preferred_element_type=jnp.float32
        ).reshape(share, rows, 2 * HEAD)
        top = mix_ref[g, s] * keep + mixed[..., :HEAD]
        bottom = sum_ref[g, s] * keep + mixed[..., HEAD:]
        result = (top / bottom * live_row[None]).astype(jnp.bfloat16)
        for j in range(share):
            attn_ref[s, :, (g * share + j) * HEAD : (g * share + j + 1) * HEAD] = result[j]


def finish(live, sent, came, up, base, query, cached, groups, size, cols):
    steps, rows, _ = query.shape
    return pl.pallas_call(
        functools.partial(final_kernel, groups, size, cols),
        out_shape=[
            jax.ShapeDtypeStruct((steps, rows, base.shape[1]), jnp.bfloat16),
            jax.ShapeDtypeStruct(query.shape, jnp.bfloat16),
        ],
        in_specs=[VMEM] * 9,
        out_specs=[VMEM] * 2,
        scratch_shapes=[pltpu.VMEM(up.shape, up.dtype)],
        compiler_params=pltpu.CompilerParams(vmem_limit_bytes=8 << 20),
        name="finish",
    )(live, sent, came, up, base, query, *cached)


def local(
    hidden, query, kv_weight, down_store, up_store, kv_cache, cache_len, block_adapter, block_fill
):
    serve = lax.axis_size("serve")
    rows = hidden.shape[1]
    size = BLK // rows
    groups = serve // size
    both = ("serve", "tensor")

    def crossing(d):
        return [(i * 2 + t, (i ^ d) * 2 + 1 - t) for i in range(serve) for t in range(2)]

    live, bias, *packed = pack(
        block_adapter, block_fill, cache_len, down_store, up_store, query, kv_cache, groups, size
    )
    if groups == 2:
        other, own = packed
        arrived = jnp.stack([own, lax.ppermute(other, both, crossing(size))])
    else:
        same = [[g * size + j for g in range(groups)] for j in range(size)]
        arrived = lax.all_to_all(packed[0], "serve", 0, 0, axis_index_groups=same, tiled=True)
    *cached, head = cache_attention(bias, query, kv_cache, kv_weight)
    arrived, cached, head, hidden = lax.optimization_barrier((arrived, cached, head, hidden))
    parts = [arrived]
    for d in range(1, size):
        parts.append(lax.ppermute(arrived, both, crossing(d)))
    base = base_projection(hidden, head, kv_weight)
    parts, base = lax.optimization_barrier((parts, base))
    sent, up = shrink(hidden, parts, groups, size)
    came = lax.ppermute(sent, "tensor", [(0, 1), (1, 0)])
    return tuple(finish(live, sent, came, up, base, query, cached, groups, size, up_store.shape[1]))


def solution(mesh):
    in_specs = (
        P(None, ("parts", "serve"), None),
        P(None, ("parts", "serve"), "tensor"),
        P(None, "tensor"),
        P("tensor", None, "serve"),
        P("tensor", "serve", None),
        P(("parts", "serve"), None, "tensor"),
        P(("parts", "serve")),
        P("parts"),
        P("parts"),
    )
    out_specs = (P(None, ("parts", "serve"), "tensor"), P(None, ("parts", "serve"), "tensor"))
    return jax.shard_map(local, mesh=mesh, in_specs=in_specs, out_specs=out_specs, check_vma=False)
```

```python
import functools
import math

import jax
import jax.numpy as jnp
from jax import lax
from jax.experimental import pallas as pl
from jax.experimental.pallas import tpu as pltpu
from jax.sharding import PartitionSpec as P

HEAD = 128
RANK = 16
BLK = 128
LANES = 128
ADAPTER_SCALE = 2.0
ROW_GROUP = 8
CHUNK = 1024
HEAD_CHUNKS = 3
EXP_SCALE = HEAD ** (-0.5) * math.log2(math.e)

HBM = pl.BlockSpec(memory_space=pl.ANY)
SMEM = pl.BlockSpec(memory_space=pltpu.SMEM)
VMEM = pl.BlockSpec(memory_space=pltpu.VMEM)


def dot_t(a, b):
    return lax.dot_general(a, b, (((1,), (1,)), ((), ())), preferred_element_type=jnp.float32)


def pack_kernel(
    groups, size, positions, ids_ref, fill_ref, len_ref, down_ref, up_ref, live_out, bias_out, *rest,
):
    out_refs, (ids, fill, lengths, window, small_sem, down_sem, up_sem) = rest[:-7], rest[-7:]
    serve = lax.axis_index("serve")
    rows = bias_out.shape[0]
    small = [
        pltpu.make_async_copy(source, target, small_sem.at[k])
        for k, (source, target) in enumerate(((ids_ref, ids), (fill_ref, fill), (len_ref, lengths)))
    ]
    for copy in small:
        copy.start()
    small[0].wait()
    first = serve // size if groups == 2 else 0
    width = down_ref.shape[2]
    cols = up_ref.shape[1]
    copies = []
    starts = []
    for k in range(groups):
        adapter = ids[lax.rem(first + groups - 1 + k, groups)]
        out = out_refs[k] if groups == 2 else out_refs[0].at[(groups - 1 + k) % groups]
        down = pltpu.make_async_copy(
            down_ref.at[0, pl.ds(pl.multiple_of(adapter * RANK, RANK), RANK), :],
            out.at[:, pl.ds(0, width)],
            down_sem.at[k],
        )
        lane = adapter * RANK // LANES * LANES
        up = pltpu.make_async_copy(
            up_ref.at[0, :, pl.ds(pl.multiple_of(lane, LANES), LANES)], window.at[k], up_sem.at[k]
        )
        up.start()
        down.start()
        copies.append((down, up, out))
        starts.append(adapter * RANK - lane)
    small[1].wait()
    small[2].wait()
    total = live_out.shape[0]
    row = lax.broadcasted_iota(jnp.int32, (total, LANES), 0) % rows + lax.rem(serve, size) * rows
    live_out[...] = (row < fill[serve // size]).astype(jnp.float32)
    wide = bias_out.shape[1]
    lanes = lax.broadcasted_iota(jnp.int32, (ROW_GROUP, wide), 1)
    subs = lax.broadcasted_iota(jnp.int32, (ROW_GROUP, wide), 0)
    start = subs * positions
    for at in range(0, rows, ROW_GROUP):
        used = jnp.zeros((ROW_GROUP, wide), jnp.int32)
        for r in range(ROW_GROUP):
            used = jnp.where(subs == r, lengths[at + r], used)
        bias_out[at : at + ROW_GROUP, :] = jnp.where((lanes >= start) & (lanes < start + used), 0.0, -jnp.inf)
    ranks = lax.broadcasted_iota(jnp.int32, (RANK, LANES), 0)
    lanes = lax.broadcasted_iota(jnp.int32, (RANK, LANES), 1)
    chosen = [(lanes == ranks + start).astype(jnp.bfloat16) for start in starts]
    for _, up, _ in copies:
        up.wait()
    picked = [dot_t(chosen[k], jnp.concatenate([window[k]] * (LANES // cols), axis=0)) for k in range(groups)]
    for k in range(groups):
        copies[k][2][:, width : width + LANES] = picked[k].astype(jnp.bfloat16)
    for down, _, _ in copies:
        down.wait()


def pack(block_adapter, block_fill, cache_len, down_store, up_store, query, kv_cache, groups, size):
    width = down_store.shape[2] + LANES
    cols = up_store.shape[1]
    steps, rows, _ = query.shape
    if groups == 2:
        messages = [jax.ShapeDtypeStruct((RANK, width), jnp.bfloat16)] * 2
    else:
        messages = [jax.ShapeDtypeStruct((groups, RANK, width), jnp.bfloat16)]
    operands = (block_adapter, block_fill, cache_len, down_store, up_store)
    return pl.pallas_call(
        functools.partial(pack_kernel, groups, size, kv_cache.shape[1]),
        out_shape=[
            jax.ShapeDtypeStruct((steps * rows, LANES), jnp.float32),
            jax.ShapeDtypeStruct((rows, ROW_GROUP * kv_cache.shape[1]), jnp.float32),
            *messages,
        ],
        in_specs=[HBM] * len(operands),
        out_specs=[VMEM] * (2 + len(messages)),
        scratch_shapes=[
            pltpu.SMEM(block_adapter.shape, jnp.int32),
            pltpu.SMEM(block_fill.shape, jnp.int32),
            pltpu.SMEM(cache_len.shape, jnp.int32),
            pltpu.VMEM((groups, cols, LANES), jnp.bfloat16),
            pltpu.SemaphoreType.DMA((3,)),
            pltpu.SemaphoreType.DMA((groups,)),
            pltpu.SemaphoreType.DMA((groups,)),
        ],
        compiler_params=pltpu.CompilerParams(vmem_limit_bytes=4 << 20),
        name="pack",
    )(*(pltpu.with_memory_space_constraint(x, pltpu.HBM) for x in operands))


def base_kernel(hidden_ref, head_ref, weight_hbm, base_ref, tail_ref, tail_sem):
    steps, rows, _ = hidden_ref.shape
    head = head_ref.shape[0]
    chunks = tail_sem.shape[0]

    def tail(i):
        at = pl.multiple_of(i * CHUNK, CHUNK)
        source = weight_hbm.at[pl.ds(pl.multiple_of(head + i * CHUNK, CHUNK), CHUNK)]
        return pltpu.make_async_copy(source, tail_ref.at[pl.ds(at, CHUNK)], tail_sem.at[i])

    for i in range(chunks):
        tail(i).start()
    states = hidden_ref[:, :, :head].reshape(steps * rows, head)
    base_ref[...] = jnp.dot(states, head_ref[...], preferred_element_type=jnp.float32)

    def step(i, carry):
        tail(i).wait()
        states = hidden_ref[:, :, pl.ds(pl.multiple_of(head + i * CHUNK, CHUNK), CHUNK)]
        part = tail_ref[pl.ds(pl.multiple_of(i * CHUNK, CHUNK), CHUNK), :]
        base_ref[...] += jnp.dot(states.reshape(steps * rows, CHUNK), part, preferred_element_type=jnp.float32)
        return carry

    lax.fori_loop(0, chunks, step, 0)


def base_projection(hidden, head, kv_weight):
    steps, rows, width = hidden.shape
    cols = kv_weight.shape[1]
    chunks = (width - head.shape[0]) // CHUNK
    return pl.pallas_call(
        base_kernel,
        out_shape=jax.ShapeDtypeStruct((steps * rows, cols), jnp.float32),
        in_specs=[VMEM, VMEM, HBM],
        out_specs=VMEM,
        scratch_shapes=[
            pltpu.VMEM((chunks * CHUNK, cols), kv_weight.dtype),
            pltpu.SemaphoreType.DMA((chunks,)),
        ],
        cost_estimate=pl.CostEstimate(
            flops=2 * steps * rows * width * cols,
            bytes_accessed=2 * width * cols + 2 * steps * rows * width,
            transcendentals=0,
        ),
        compiler_params=pltpu.CompilerParams(vmem_limit_bytes=14 << 20),
        name="base",
    )(hidden, head, pltpu.with_memory_space_constraint(kv_weight, pltpu.HBM))


def cache_kernel(bias_ref, query_ref, cache_ref, weight_hbm, mix_ref, sum_ref, max_ref, head_ref, head_sem):
    head_copy = pltpu.make_async_copy(weight_hbm.at[pl.ds(0, head_ref.shape[0])], head_ref, head_sem)
    head_copy.start()
    steps, rows, _ = query_ref.shape
    positions = cache_ref.shape[1]
    kv_heads = cache_ref.shape[2] // (2 * HEAD)
    share = query_ref.shape[2] // (kv_heads * HEAD)
    wide = ROW_GROUP * positions
    ones = jnp.ones((wide, HEAD), jnp.bfloat16)

    def pair(p, carry):
        first = pl.multiple_of(p * 2 * ROW_GROUP, 2 * ROW_GROUP)
        for half in range(2):
            own = pl.ds(pl.multiple_of(first + half * ROW_GROUP, ROW_GROUP), ROW_GROUP)
            bias = bias_ref[own, :]
            for g in range(kv_heads):
                stored = cache_ref[own, :, g * 2 * HEAD : (g + 1) * 2 * HEAD].reshape(wide, 2 * HEAD)
                parts = []
                for s in range(steps):
                    for j in range(share):
                        at = (g * share + j) * HEAD
                        both = query_ref[s, pl.ds(first, 2 * ROW_GROUP), at : at + HEAD]
                        both = both.astype(jnp.float32)
                        parts.append(both[half * ROW_GROUP : (half + 1) * ROW_GROUP])
                stacked = jnp.concatenate(parts, axis=0).astype(jnp.bfloat16)
                scores = dot_t(stacked, stored[:, :HEAD]).reshape(steps * share, ROW_GROUP, wide)
                scores = scores + bias[None]
                highest = jnp.max(scores, axis=-1, keepdims=True)
                weights = jnp.exp2((scores - highest) * EXP_SCALE).reshape(-1, wide).astype(jnp.bfloat16)
                values = jnp.concatenate([stored[:, HEAD:], ones], axis=1)
                mixed = jnp.dot(weights, values, preferred_element_type=jnp.float32)
                mixed = mixed.reshape(steps, share, ROW_GROUP, 2 * HEAD)
                mix_ref[g, :, :, own, :] = mixed[..., :HEAD]
                sum_ref[g, :, :, own, :] = mixed[..., HEAD:]
                max_ref[g, :, :, own, :] = jnp.broadcast_to(
                    highest.reshape(steps, share, ROW_GROUP, 1), (steps, share, ROW_GROUP, HEAD)
                )
        return carry

    lax.fori_loop(0, rows // (2 * ROW_GROUP), pair, 0)
    head_copy.wait()


def cache_attention(bias, query, kv_cache, kv_weight):
    steps, rows, heads_width = query.shape
    kv_heads = kv_cache.shape[2] // (2 * HEAD)
    share = heads_width // (kv_heads * HEAD)
    head = jax.ShapeDtypeStruct((HEAD_CHUNKS * CHUNK, kv_weight.shape[1]), kv_weight.dtype)
    shape = jax.ShapeDtypeStruct((kv_heads, steps, share, rows, HEAD), jnp.float32)
    return pl.pallas_call(
        cache_kernel,
        out_shape=[shape] * 3 + [head],
        in_specs=[VMEM] * 3 + [HBM],
        out_specs=[VMEM] * 4,
        scratch_shapes=[pltpu.SemaphoreType.DMA],
        cost_estimate=pl.CostEstimate(
            flops=40 * 2 * 2 * steps * heads_width * rows * ROW_GROUP * kv_cache.shape[1],
            bytes_accessed=2 * kv_cache.size,
            transcendentals=0,
        ),
        compiler_params=pltpu.CompilerParams(vmem_limit_bytes=12 << 20),
        name="cached",
    )(bias, query, kv_cache, pltpu.with_memory_space_constraint(kv_weight, pltpu.HBM))


def pieces(groups, size):
    return [(e, d, ((groups == 2 and e == 1) != (d > 0))) for d in range(size) for e in range(groups)]


def piece_source(groups, size, e, d):
    me = lax.axis_index("serve")
    first = me // size if groups == 2 else 0
    return lax.rem(first + e, groups) * size + (lax.rem(me, size) ^ d)


def shrink_kernel(groups, size, cols, hidden_ref, *rest):
    part_refs, (send_ref, up_ref) = rest[:-2], rest[-2:]
    steps, rows, _ = hidden_ref.shape
    total = steps * rows
    width = (part_refs[0].shape[1] - LANES) // groups
    sums = [jnp.zeros((total, RANK), jnp.float32)] * 2
    at = 2 * total
    for e, d, crossed in pieces(groups, size):
        source = piece_source(groups, size, e, d)
        states = hidden_ref[:, :, pl.ds(pl.multiple_of(source * width, LANES), width)]
        factors = part_refs[d][:, e * width : (e + 1) * width]
        sums[crossed] = sums[crossed] + dot_t(states.reshape(total, width), factors)
        shift = lax.rem((lax.rem(source, LANES // cols) - e) * cols + LANES, LANES)
        up = pltpu.roll(part_refs[d][:, groups * width :].astype(jnp.float32), shift, 1)
        if crossed:
            send_ref[at : at + RANK, :] = up
            at += RANK
        else:
            up_ref[source] = up.astype(jnp.bfloat16)
    send_ref[:total, :RANK] = sums[0]
    send_ref[total : 2 * total, :RANK] = sums[1]


def shrink(hidden, parts, groups, size, cols):
    steps, rows, _ = hidden.shape
    crossed = sum(c for _, _, c in pieces(groups, size))
    return pl.pallas_call(
        functools.partial(shrink_kernel, groups, size, cols),
        out_shape=[
            jax.ShapeDtypeStruct((2 * steps * rows + crossed * RANK, LANES), jnp.float32),
            jax.ShapeDtypeStruct((groups * size, RANK, LANES), jnp.bfloat16),
        ],
        in_specs=[VMEM] * (1 + len(parts)),
        out_specs=[VMEM] * 2,
        compiler_params=pltpu.CompilerParams(vmem_limit_bytes=4 << 20),
        name="shrink",
    )(hidden, *parts)


def final_kernel(
    groups, size, cols, live_ref, sent_ref, came_ref, straight_ref, base_ref, query_ref, mix_ref, sum_ref, max_ref,
    new_ref, attn_ref, up_ref,
):
    steps, rows, _ = query_ref.shape
    kv_heads, _, share = mix_ref.shape[:3]
    total = steps * rows
    live = live_ref[...]
    core = lax.axis_index("tensor")
    own_sum = sent_ref[:total, :RANK] + came_ref[total : 2 * total, :RANK]
    other_sum = sent_ref[total : 2 * total, :RANK] + came_ref[:total, :RANK]
    keys_low = (live[:, :RANK] * jnp.where(core == 0, own_sum, other_sum)).astype(jnp.bfloat16)
    values_low = (live[:, :RANK] * jnp.where(core == 0, other_sum, own_sum)).astype(jnp.bfloat16)
    at = 2 * total
    for e, d, crossed in pieces(groups, size):
        source = piece_source(groups, size, e, d)
        if crossed:
            up_ref[source] = came_ref[at : at + RANK, :].astype(jnp.bfloat16)
            at += RANK
        else:
            up_ref[source] = straight_ref[source]
    lane = lax.broadcasted_iota(jnp.int32, (RANK, LANES), 1)
    each = LANES // cols
    query_row = lax.broadcasted_iota(jnp.int32, (total, total), 0)
    key_row = lax.broadcasted_iota(jnp.int32, (total, total), 1)
    seen = (query_row % rows == key_row % rows) & (key_row // rows <= query_row // rows)
    bias = jnp.where(seen, 0.0, -jnp.inf).reshape(steps, 1, rows, total)
    ones = jnp.ones((total, HEAD), jnp.bfloat16)
    live_row = live[:rows]
    fresh = []
    for tile in range(2 * kv_heads):
        up = up_ref[tile * each]
        for k in range(1, each):
            up = jnp.where(lane // cols == k, up_ref[tile * each + k], up)
        low = keys_low if tile % 2 == 0 else values_low
        delta = jnp.dot(low, up, preferred_element_type=jnp.float32)
        at = slice(tile * HEAD, (tile + 1) * HEAD)
        value = (live * (base_ref[:, at] + ADAPTER_SCALE * delta)).astype(jnp.bfloat16)
        new_ref[:, :, at] = value.reshape(steps, rows, HEAD)
        fresh.append(value)
    todo = [(g, s) for g in range(kv_heads) for s in range(steps)]
    found = []
    for g, s in todo:
        queries = jnp.concatenate(
            [query_ref[s, :, (g * share + j) * HEAD : (g * share + j + 1) * HEAD] for j in range(share)], axis=0
        )
        scores = dot_t(queries, fresh[2 * g]).reshape(share, rows, total) + bias[s]
        found.append((scores, jnp.max(scores, axis=-1, keepdims=True)))
    for (g, s), (scores, most) in zip(todo, found):
        cached_max = max_ref[g, s]
        highest = jnp.maximum(cached_max, most)
        weights = jnp.exp2((scores - highest[:, :, :total]) * EXP_SCALE)
        keep = jnp.exp2((cached_max - highest) * EXP_SCALE)
        values = jnp.concatenate([fresh[2 * g + 1], ones], axis=1)
        mixed = jnp.dot(
            weights.reshape(-1, total).astype(jnp.bfloat16), values, preferred_element_type=jnp.float32
        ).reshape(share, rows, 2 * HEAD)
        top = mix_ref[g, s] * keep + mixed[..., :HEAD]
        bottom = sum_ref[g, s] * keep + mixed[..., HEAD:]
        result = (top / bottom * live_row[None]).astype(jnp.bfloat16)
        for j in range(share):
            attn_ref[s, :, (g * share + j) * HEAD : (g * share + j + 1) * HEAD] = result[j]


def finish(live, sent, came, up, base, query, cached, groups, size, cols):
    steps, rows, _ = query.shape
    return pl.pallas_call(
        functools.partial(final_kernel, groups, size, cols),
        out_shape=[
            jax.ShapeDtypeStruct((steps, rows, base.shape[1]), jnp.bfloat16),
            jax.ShapeDtypeStruct(query.shape, jnp.bfloat16),
        ],
        in_specs=[VMEM] * 9,
        out_specs=[VMEM] * 2,
        scratch_shapes=[pltpu.VMEM(up.shape, up.dtype)],
        compiler_params=pltpu.CompilerParams(vmem_limit_bytes=8 << 20),
        name="finish",
    )(live, sent, came, up, base, query, *cached)


def join(slices, cols):
    run = jnp.arange(LANES)[None, :] // cols
    up = slices[0][:, -LANES:]
    for e, part in enumerate(slices[1:], 1):
        up = jnp.where(run == e, part[:, -LANES:], up)
    return jnp.concatenate([part[:, :-LANES] for part in slices] + [up], axis=1)


def local(
    hidden, query, kv_weight, down_store, up_store, kv_cache, cache_len, block_adapter, block_fill
):
    serve = lax.axis_size("serve")
    rows = hidden.shape[1]
    size = BLK // rows
    groups = serve // size
    both = ("serve", "tensor")

    def crossing(d):
        return [(i * 2 + t, (i ^ d) * 2 + 1 - t) for i in range(serve) for t in range(2)]

    live, bias, *packed = pack(
        block_adapter, block_fill, cache_len, down_store, up_store, query, kv_cache, groups, size
    )
    if groups == 2:
        other, own = packed
        slices = [own, lax.ppermute(other, both, crossing(size))]
    else:
        same = [[g * size + j for g in range(groups)] for j in range(size)]
        slices = list(lax.all_to_all(packed[0], "serve", 0, 0, axis_index_groups=same, tiled=True))
    arrived = join(slices, up_store.shape[1])
    *cached, head = cache_attention(bias, query, kv_cache, kv_weight)
    arrived, cached, head, hidden = lax.optimization_barrier((arrived, cached, head, hidden))
    parts = [arrived]
    for d in range(1, size):
        parts.append(lax.ppermute(arrived, both, crossing(d)))
    base = base_projection(hidden, head, kv_weight)
    parts, base = lax.optimization_barrier((parts, base))
    sent, up = shrink(hidden, parts, groups, size, up_store.shape[1])
    came = lax.ppermute(sent, "tensor", [(0, 1), (1, 0)])
    return tuple(finish(live, sent, came, up, base, query, cached, groups, size, up_store.shape[1]))


def solution(mesh):
    in_specs = (
        P(None, ("parts", "serve"), None),
        P(None, ("parts", "serve"), "tensor"),
        P(None, "tensor"),
        P("tensor", None, "serve"),
        P("tensor", "serve", None),
        P(("parts", "serve"), None, "tensor"),
        P(("parts", "serve")),
        P("parts"),
        P("parts"),
    )
    out_specs = (P(None, ("parts", "serve"), "tensor"), P(None, ("parts", "serve"), "tensor"))
    return jax.shard_map(local, mesh=mesh, in_specs=in_specs, out_specs=out_specs, check_vma=False)
```

```python
import functools
import math

import jax
import jax.numpy as jnp
from jax import lax
from jax.experimental import pallas as pl
from jax.experimental.pallas import tpu as pltpu
from jax.sharding import PartitionSpec as P

HEAD = 128
RANK = 16
BLK = 128
LANES = 128
ADAPTER_SCALE = 2.0
ROW_GROUP = 8
CHUNK = 1024
HEAD_CHUNKS = 3
EXP_SCALE = HEAD ** (-0.5) * math.log2(math.e)

HBM = pl.BlockSpec(memory_space=pl.ANY)
SMEM = pl.BlockSpec(memory_space=pltpu.SMEM)
VMEM = pl.BlockSpec(memory_space=pltpu.VMEM)


def dot_t(a, b):
    return lax.dot_general(a, b, (((1,), (1,)), ((), ())), preferred_element_type=jnp.float32)


def pack_kernel(
    groups, size, positions, ids_ref, fill_ref, len_ref, down_ref, up_ref, live_out, bias_out, *rest,
):
    out_refs, (ids, fill, lengths, window, small_sem, down_sem, up_sem) = rest[:-7], rest[-7:]
    serve = lax.axis_index("serve")
    rows = bias_out.shape[0]
    small = [
        pltpu.make_async_copy(source, target, small_sem.at[k])
        for k, (source, target) in enumerate(((ids_ref, ids), (fill_ref, fill), (len_ref, lengths)))
    ]
    for copy in small:
        copy.start()
    small[0].wait()
    first = serve // size if groups == 2 else 0
    width = down_ref.shape[2]
    cols = up_ref.shape[1]
    copies = []
    starts = []
    for k in range(groups):
        adapter = ids[lax.rem(first + groups - 1 + k, groups)]
        out = out_refs[k] if groups == 2 else out_refs[0].at[(groups - 1 + k) % groups]
        down = pltpu.make_async_copy(
            down_ref.at[0, pl.ds(pl.multiple_of(adapter * RANK, RANK), RANK), :],
            out.at[:, pl.ds(0, width)],
            down_sem.at[k],
        )
        lane = adapter * RANK // LANES * LANES
        up = pltpu.make_async_copy(
            up_ref.at[0, :, pl.ds(pl.multiple_of(lane, LANES), LANES)], window.at[k], up_sem.at[k]
        )
        up.start()
        down.start()
        copies.append((down, up, out))
        starts.append(adapter * RANK - lane)
    small[1].wait()
    small[2].wait()
    total = live_out.shape[0]
    row = lax.broadcasted_iota(jnp.int32, (total, LANES), 0) % rows + lax.rem(serve, size) * rows
    live_out[...] = (row < fill[serve // size]).astype(jnp.float32)
    wide = bias_out.shape[1]
    lanes = lax.broadcasted_iota(jnp.int32, (ROW_GROUP, wide), 1)
    subs = lax.broadcasted_iota(jnp.int32, (ROW_GROUP, wide), 0)
    start = subs * positions
    for at in range(0, rows, ROW_GROUP):
        used = jnp.zeros((ROW_GROUP, wide), jnp.int32)
        for r in range(ROW_GROUP):
            used = jnp.where(subs == r, lengths[at + r], used)
        bias_out[at : at + ROW_GROUP, :] = jnp.where((lanes >= start) & (lanes < start + used), 0.0, -jnp.inf)
    ranks = lax.broadcasted_iota(jnp.int32, (RANK, LANES), 0)
    lanes = lax.broadcasted_iota(jnp.int32, (RANK, LANES), 1)
    chosen = [(lanes == ranks + start).astype(jnp.bfloat16) for start in starts]
    for _, up, _ in copies:
        up.wait()
    picked = [dot_t(chosen[k], jnp.concatenate([window[k]] * (LANES // cols), axis=0)) for k in range(groups)]
    for k in range(groups):
        copies[k][2][:, width : width + LANES] = picked[k].astype(jnp.bfloat16)
    for down, _, _ in copies:
        down.wait()


def pack(block_adapter, block_fill, cache_len, down_store, up_store, query, kv_cache, groups, size):
    width = down_store.shape[2] + LANES
    cols = up_store.shape[1]
    steps, rows, _ = query.shape
    if groups == 2:
        messages = [jax.ShapeDtypeStruct((RANK, width), jnp.bfloat16)] * 2
    else:
        messages = [jax.ShapeDtypeStruct((groups, RANK, width), jnp.bfloat16)]
    operands = (block_adapter, block_fill, cache_len, down_store, up_store)
    return pl.pallas_call(
        functools.partial(pack_kernel, groups, size, kv_cache.shape[1]),
        out_shape=[
            jax.ShapeDtypeStruct((steps * rows, LANES), jnp.float32),
            jax.ShapeDtypeStruct((rows, ROW_GROUP * kv_cache.shape[1]), jnp.float32),
            *messages,
        ],
        in_specs=[HBM] * len(operands),
        out_specs=[VMEM] * (2 + len(messages)),
        scratch_shapes=[
            pltpu.SMEM(block_adapter.shape, jnp.int32),
            pltpu.SMEM(block_fill.shape, jnp.int32),
            pltpu.SMEM(cache_len.shape, jnp.int32),
            pltpu.VMEM((groups, cols, LANES), jnp.bfloat16),
            pltpu.SemaphoreType.DMA((3,)),
            pltpu.SemaphoreType.DMA((groups,)),
            pltpu.SemaphoreType.DMA((groups,)),
        ],
        compiler_params=pltpu.CompilerParams(vmem_limit_bytes=4 << 20),
        name="pack",
    )(*(pltpu.with_memory_space_constraint(x, pltpu.HBM) for x in operands))


def base_kernel(hidden_ref, head_ref, weight_hbm, base_ref, tail_ref, tail_sem):
    steps, rows, _ = hidden_ref.shape
    head = head_ref.shape[0]
    chunks = tail_sem.shape[0]

    def tail(i):
        at = pl.multiple_of(i * CHUNK, CHUNK)
        source = weight_hbm.at[pl.ds(pl.multiple_of(head + i * CHUNK, CHUNK), CHUNK)]
        return pltpu.make_async_copy(source, tail_ref.at[pl.ds(at, CHUNK)], tail_sem.at[i])

    for i in range(chunks):
        tail(i).start()
    states = hidden_ref[:, :, :head].reshape(steps * rows, head)
    base_ref[...] = jnp.dot(states, head_ref[...], preferred_element_type=jnp.float32)

    def step(i, carry):
        tail(i).wait()
        states = hidden_ref[:, :, pl.ds(pl.multiple_of(head + i * CHUNK, CHUNK), CHUNK)]
        part = tail_ref[pl.ds(pl.multiple_of(i * CHUNK, CHUNK), CHUNK), :]
        base_ref[...] += jnp.dot(states.reshape(steps * rows, CHUNK), part, preferred_element_type=jnp.float32)
        return carry

    lax.fori_loop(0, chunks, step, 0)


def base_projection(hidden, head, kv_weight):
    steps, rows, width = hidden.shape
    cols = kv_weight.shape[1]
    chunks = (width - head.shape[0]) // CHUNK
    return pl.pallas_call(
        base_kernel,
        out_shape=jax.ShapeDtypeStruct((steps * rows, cols), jnp.float32),
        in_specs=[VMEM, VMEM, HBM],
        out_specs=VMEM,
        scratch_shapes=[
            pltpu.VMEM((chunks * CHUNK, cols), kv_weight.dtype),
            pltpu.SemaphoreType.DMA((chunks,)),
        ],
        cost_estimate=pl.CostEstimate(
            flops=2 * steps * rows * width * cols,
            bytes_accessed=2 * width * cols + 2 * steps * rows * width,
            transcendentals=0,
        ),
        compiler_params=pltpu.CompilerParams(vmem_limit_bytes=14 << 20),
        name="base",
    )(hidden, head, pltpu.with_memory_space_constraint(kv_weight, pltpu.HBM))


def cache_kernel(bias_ref, query_ref, cache_ref, weight_hbm, mix_ref, sum_ref, max_ref, head_ref, head_sem):
    head_copy = pltpu.make_async_copy(weight_hbm.at[pl.ds(0, head_ref.shape[0])], head_ref, head_sem)
    head_copy.start()
    steps, rows, _ = query_ref.shape
    positions = cache_ref.shape[1]
    kv_heads = cache_ref.shape[2] // (2 * HEAD)
    share = query_ref.shape[2] // (kv_heads * HEAD)
    wide = ROW_GROUP * positions
    ones = jnp.ones((wide, HEAD), jnp.bfloat16)

    def pair(p, carry):
        first = pl.multiple_of(p * 2 * ROW_GROUP, 2 * ROW_GROUP)
        for half in range(2):
            own = pl.ds(pl.multiple_of(first + half * ROW_GROUP, ROW_GROUP), ROW_GROUP)
            bias = bias_ref[own, :]
            for g in range(kv_heads):
                stored = cache_ref[own, :, g * 2 * HEAD : (g + 1) * 2 * HEAD].reshape(wide, 2 * HEAD)
                parts = []
                for s in range(steps):
                    for j in range(share):
                        at = (g * share + j) * HEAD
                        both = query_ref[s, pl.ds(first, 2 * ROW_GROUP), at : at + HEAD]
                        both = both.astype(jnp.float32)
                        parts.append(both[half * ROW_GROUP : (half + 1) * ROW_GROUP])
                stacked = jnp.concatenate(parts, axis=0).astype(jnp.bfloat16)
                scores = dot_t(stacked, stored[:, :HEAD]).reshape(steps * share, ROW_GROUP, wide)
                scores = scores + bias[None]
                highest = jnp.max(scores, axis=-1, keepdims=True)
                weights = jnp.exp2((scores - highest) * EXP_SCALE).reshape(-1, wide).astype(jnp.bfloat16)
                values = jnp.concatenate([stored[:, HEAD:], ones], axis=1)
                mixed = jnp.dot(weights, values, preferred_element_type=jnp.float32)
                mixed = mixed.reshape(steps, share, ROW_GROUP, 2 * HEAD)
                mix_ref[g, :, :, own, :] = mixed[..., :HEAD]
                sum_ref[g, :, :, own, :] = mixed[..., HEAD:]
                max_ref[g, :, :, own, :] = jnp.broadcast_to(
                    highest.reshape(steps, share, ROW_GROUP, 1), (steps, share, ROW_GROUP, HEAD)
                )
        return carry

    lax.fori_loop(0, rows // (2 * ROW_GROUP), pair, 0)
    head_copy.wait()


def cache_attention(bias, query, kv_cache, kv_weight):
    steps, rows, heads_width = query.shape
    kv_heads = kv_cache.shape[2] // (2 * HEAD)
    share = heads_width // (kv_heads * HEAD)
    head = jax.ShapeDtypeStruct((HEAD_CHUNKS * CHUNK, kv_weight.shape[1]), kv_weight.dtype)
    shape = jax.ShapeDtypeStruct((kv_heads, steps, share, rows, HEAD), jnp.float32)
    return pl.pallas_call(
        cache_kernel,
        out_shape=[shape] * 3 + [head],
        in_specs=[VMEM] * 3 + [HBM],
        out_specs=[VMEM] * 4,
        scratch_shapes=[pltpu.SemaphoreType.DMA],
        cost_estimate=pl.CostEstimate(
            flops=14 * 2 * 2 * steps * heads_width * rows * ROW_GROUP * kv_cache.shape[1],
            bytes_accessed=2 * kv_cache.size,
            transcendentals=0,
        ),
        compiler_params=pltpu.CompilerParams(vmem_limit_bytes=12 << 20),
        name="cached",
    )(bias, query, kv_cache, pltpu.with_memory_space_constraint(kv_weight, pltpu.HBM))


def pieces(groups, size):
    return [(e, d, ((groups == 2 and e == 1) != (d > 0))) for d in range(size) for e in range(groups)]


def piece_source(groups, size, e, d):
    me = lax.axis_index("serve")
    first = me // size if groups == 2 else 0
    return lax.rem(first + e, groups) * size + (lax.rem(me, size) ^ d)


def shrink_kernel(groups, size, cols, hidden_ref, *rest):
    part_refs, (send_ref, up_ref) = rest[:-2], rest[-2:]
    steps, rows, _ = hidden_ref.shape
    total = steps * rows
    width = (part_refs[0].shape[1] - LANES) // groups
    sums = [jnp.zeros((total, RANK), jnp.float32)] * 2
    at = 2 * total
    for e, d, crossed in pieces(groups, size):
        source = piece_source(groups, size, e, d)
        states = hidden_ref[:, :, pl.ds(pl.multiple_of(source * width, LANES), width)]
        factors = part_refs[d][:, e * width : (e + 1) * width]
        sums[crossed] = sums[crossed] + dot_t(states.reshape(total, width), factors)
        shift = lax.rem((lax.rem(source, LANES // cols) - e) * cols + LANES, LANES)
        up = pltpu.roll(part_refs[d][:, groups * width :].astype(jnp.float32), shift, 1)
        if crossed:
            send_ref[at : at + RANK, :] = up
            at += RANK
        else:
            up_ref[source] = up.astype(jnp.bfloat16)
    send_ref[:total, :RANK] = sums[0]
    send_ref[total : 2 * total, :RANK] = sums[1]


def shrink(hidden, parts, groups, size, cols):
    steps, rows, _ = hidden.shape
    crossed = sum(c for _, _, c in pieces(groups, size))
    return pl.pallas_call(
        functools.partial(shrink_kernel, groups, size, cols),
        out_shape=[
            jax.ShapeDtypeStruct((2 * steps * rows + crossed * RANK, LANES), jnp.float32),
            jax.ShapeDtypeStruct((groups * size, RANK, LANES), jnp.bfloat16),
        ],
        in_specs=[VMEM] * (1 + len(parts)),
        out_specs=[VMEM] * 2,
        compiler_params=pltpu.CompilerParams(vmem_limit_bytes=4 << 20),
        name="shrink",
    )(hidden, *parts)


def final_kernel(
    groups, size, cols, live_ref, sent_ref, came_ref, straight_ref, base_ref, query_ref, mix_ref, sum_ref, max_ref,
    new_ref, attn_ref, up_ref,
):
    steps, rows, _ = query_ref.shape
    kv_heads, _, share = mix_ref.shape[:3]
    total = steps * rows
    live = live_ref[...]
    core = lax.axis_index("tensor")
    own_sum = sent_ref[:total, :RANK] + came_ref[total : 2 * total, :RANK]
    other_sum = sent_ref[total : 2 * total, :RANK] + came_ref[:total, :RANK]
    keys_low = (live[:, :RANK] * jnp.where(core == 0, own_sum, other_sum)).astype(jnp.bfloat16)
    values_low = (live[:, :RANK] * jnp.where(core == 0, other_sum, own_sum)).astype(jnp.bfloat16)
    at = 2 * total
    for e, d, crossed in pieces(groups, size):
        source = piece_source(groups, size, e, d)
        if crossed:
            up_ref[source] = came_ref[at : at + RANK, :].astype(jnp.bfloat16)
            at += RANK
        else:
            up_ref[source] = straight_ref[source]
    lane = lax.broadcasted_iota(jnp.int32, (RANK, LANES), 1)
    each = LANES // cols
    query_row = lax.broadcasted_iota(jnp.int32, (total, total), 0)
    key_row = lax.broadcasted_iota(jnp.int32, (total, total), 1)
    seen = (query_row % rows == key_row % rows) & (key_row // rows <= query_row // rows)
    bias = jnp.where(seen, 0.0, -jnp.inf).reshape(steps, 1, rows, total)
    ones = jnp.ones((total, HEAD), jnp.bfloat16)
    live_row = live[:rows]
    fresh = []
    for tile in range(2 * kv_heads):
        up = up_ref[tile * each]
        for k in range(1, each):
            up = jnp.where(lane // cols == k, up_ref[tile * each + k], up)
        low = keys_low if tile % 2 == 0 else values_low
        delta = jnp.dot(low, up, preferred_element_type=jnp.float32)
        at = slice(tile * HEAD, (tile + 1) * HEAD)
        value = (live * (base_ref[:, at] + ADAPTER_SCALE * delta)).astype(jnp.bfloat16)
        new_ref[:, :, at] = value.reshape(steps, rows, HEAD)
        fresh.append(value)
    todo = [(g, s) for g in range(kv_heads) for s in range(steps)]
    found = []
    for g, s in todo:
        queries = jnp.concatenate(
            [query_ref[s, :, (g * share + j) * HEAD : (g * share + j + 1) * HEAD] for j in range(share)], axis=0
        )
        scores = dot_t(queries, fresh[2 * g]).reshape(share, rows, total) + bias[s]
        found.append((scores, jnp.max(scores, axis=-1, keepdims=True)))
    for (g, s), (scores, most) in zip(todo, found):
        cached_max = max_ref[g, s]
        highest = jnp.maximum(cached_max, most)
        weights = jnp.exp2((scores - highest[:, :, :total]) * EXP_SCALE)
        keep = jnp.exp2((cached_max - highest) * EXP_SCALE)
        values = jnp.concatenate([fresh[2 * g + 1], ones], axis=1)
        mixed = jnp.dot(
            weights.reshape(-1, total).astype(jnp.bfloat16), values, preferred_element_type=jnp.float32
        ).reshape(share, rows, 2 * HEAD)
        top = mix_ref[g, s] * keep + mixed[..., :HEAD]
        bottom = sum_ref[g, s] * keep + mixed[..., HEAD:]
        result = (top / bottom * live_row[None]).astype(jnp.bfloat16)
        for j in range(share):
            attn_ref[s, :, (g * share + j) * HEAD : (g * share + j + 1) * HEAD] = result[j]


def finish(live, sent, came, up, base, query, cached, groups, size, cols):
    steps, rows, _ = query.shape
    return pl.pallas_call(
        functools.partial(final_kernel, groups, size, cols),
        out_shape=[
            jax.ShapeDtypeStruct((steps, rows, base.shape[1]), jnp.bfloat16),
            jax.ShapeDtypeStruct(query.shape, jnp.bfloat16),
        ],
        in_specs=[VMEM] * 9,
        out_specs=[VMEM] * 2,
        scratch_shapes=[pltpu.VMEM(up.shape, up.dtype)],
        compiler_params=pltpu.CompilerParams(vmem_limit_bytes=8 << 20),
        name="finish",
    )(live, sent, came, up, base, query, *cached)


def join(slices, cols):
    run = jnp.arange(LANES)[None, :] // cols
    up = slices[0][:, -LANES:]
    for e, part in enumerate(slices[1:], 1):
        up = jnp.where(run == e, part[:, -LANES:], up)
    return jnp.concatenate([part[:, :-LANES] for part in slices] + [up], axis=1)


def local(
    hidden, query, kv_weight, down_store, up_store, kv_cache, cache_len, block_adapter, block_fill
):
    serve = lax.axis_size("serve")
    rows = hidden.shape[1]
    size = BLK // rows
    groups = serve // size
    both = ("serve", "tensor")

    def crossing(d):
        return [(i * 2 + t, (i ^ d) * 2 + 1 - t) for i in range(serve) for t in range(2)]

    live, bias, *packed = pack(
        block_adapter, block_fill, cache_len, down_store, up_store, query, kv_cache, groups, size
    )
    if groups == 2:
        other, own = packed
        slices = [own, lax.ppermute(other, both, crossing(size))]
    else:
        same = [[g * size + j for g in range(groups)] for j in range(size)]
        slices = list(lax.all_to_all(packed[0], "serve", 0, 0, axis_index_groups=same, tiled=True))
    arrived = join(slices, up_store.shape[1])
    *cached, head = cache_attention(bias, query, kv_cache, kv_weight)
    arrived, cached, head, hidden = lax.optimization_barrier((arrived, cached, head, hidden))
    parts = [arrived]
    for d in range(1, size):
        parts.append(lax.ppermute(arrived, both, crossing(d)))
    base = base_projection(hidden, head, kv_weight)
    parts, base = lax.optimization_barrier((parts, base))
    sent, up = shrink(hidden, parts, groups, size, up_store.shape[1])
    came = lax.ppermute(sent, "tensor", [(0, 1), (1, 0)])
    return tuple(finish(live, sent, came, up, base, query, cached, groups, size, up_store.shape[1]))


def solution(mesh):
    in_specs = (
        P(None, ("parts", "serve"), None),
        P(None, ("parts", "serve"), "tensor"),
        P(None, "tensor"),
        P("tensor", None, "serve"),
        P("tensor", "serve", None),
        P(("parts", "serve"), None, "tensor"),
        P(("parts", "serve")),
        P("parts"),
        P("parts"),
    )
    out_specs = (P(None, ("parts", "serve"), "tensor"), P(None, ("parts", "serve"), "tensor"))
    return jax.shard_map(local, mesh=mesh, in_specs=in_specs, out_specs=out_specs, check_vma=False)
```

```python
import functools
import math

import jax
import jax.numpy as jnp
from jax import lax
from jax.experimental import pallas as pl
from jax.experimental.pallas import tpu as pltpu
from jax.sharding import PartitionSpec as P

HEAD = 128
RANK = 16
BLK = 128
LANES = 128
ADAPTER_SCALE = 2.0
ROW_GROUP = 8
CHUNK = 1024
HEAD_CHUNKS = 3
EXP_SCALE = HEAD ** (-0.5) * math.log2(math.e)

HBM = pl.BlockSpec(memory_space=pl.ANY)
SMEM = pl.BlockSpec(memory_space=pltpu.SMEM)
VMEM = pl.BlockSpec(memory_space=pltpu.VMEM)


def dot_t(a, b):
    return lax.dot_general(a, b, (((1,), (1,)), ((), ())), preferred_element_type=jnp.float32)


def pack_kernel(
    groups, size, positions, ids_ref, fill_ref, len_ref, down_ref, up_ref, live_out, bias_out, *rest,
):
    out_refs, (ids, fill, lengths, window, small_sem, down_sem, up_sem) = rest[:-7], rest[-7:]
    serve = lax.axis_index("serve")
    rows = bias_out.shape[0]
    small = [
        pltpu.make_async_copy(source, target, small_sem.at[k])
        for k, (source, target) in enumerate(((ids_ref, ids), (fill_ref, fill), (len_ref, lengths)))
    ]
    for copy in small:
        copy.start()
    small[0].wait()
    first = serve // size if groups == 2 else 0
    width = down_ref.shape[2]
    cols = up_ref.shape[1]
    copies = []
    starts = []
    for k in range(groups):
        adapter = ids[lax.rem(first + groups - 1 + k, groups)]
        out = out_refs[k] if groups == 2 else out_refs[0].at[(groups - 1 + k) % groups]
        down = pltpu.make_async_copy(
            down_ref.at[0, pl.ds(pl.multiple_of(adapter * RANK, RANK), RANK), :],
            out.at[:, pl.ds(0, width)],
            down_sem.at[k],
        )
        lane = adapter * RANK // LANES * LANES
        up = pltpu.make_async_copy(
            up_ref.at[0, :, pl.ds(pl.multiple_of(lane, LANES), LANES)], window.at[k], up_sem.at[k]
        )
        up.start()
        down.start()
        copies.append((down, up, out))
        starts.append(adapter * RANK - lane)
    small[1].wait()
    small[2].wait()
    total = live_out.shape[0]
    row = lax.broadcasted_iota(jnp.int32, (total, LANES), 0) % rows + lax.rem(serve, size) * rows
    live_out[...] = (row < fill[serve // size]).astype(jnp.float32)
    wide = bias_out.shape[1]
    lanes = lax.broadcasted_iota(jnp.int32, (ROW_GROUP, wide), 1)
    subs = lax.broadcasted_iota(jnp.int32, (ROW_GROUP, wide), 0)
    start = subs * positions
    for at in range(0, rows, ROW_GROUP):
        used = jnp.zeros((ROW_GROUP, wide), jnp.int32)
        for r in range(ROW_GROUP):
            used = jnp.where(subs == r, lengths[at + r], used)
        bias_out[at : at + ROW_GROUP, :] = jnp.where((lanes >= start) & (lanes < start + used), 0.0, -jnp.inf)
    ranks = lax.broadcasted_iota(jnp.int32, (RANK, LANES), 0)
    lanes = lax.broadcasted_iota(jnp.int32, (RANK, LANES), 1)
    chosen = [(lanes == ranks + start).astype(jnp.bfloat16) for start in starts]
    for _, up, _ in copies:
        up.wait()
    picked = [dot_t(chosen[k], jnp.concatenate([window[k]] * (LANES // cols), axis=0)) for k in range(groups)]
    for k in range(groups):
        copies[k][2][:, width : width + LANES] = picked[k].astype(jnp.bfloat16)
    for down, _, _ in copies:
        down.wait()


def pack(block_adapter, block_fill, cache_len, down_store, up_store, query, kv_cache, groups, size):
    width = down_store.shape[2] + LANES
    cols = up_store.shape[1]
    steps, rows, _ = query.shape
    if groups == 2:
        messages = [jax.ShapeDtypeStruct((RANK, width), jnp.bfloat16)] * 2
    else:
        messages = [jax.ShapeDtypeStruct((groups, RANK, width), jnp.bfloat16)]
    operands = (block_adapter, block_fill, cache_len, down_store, up_store)
    return pl.pallas_call(
        functools.partial(pack_kernel, groups, size, kv_cache.shape[1]),
        out_shape=[
            jax.ShapeDtypeStruct((steps * rows, LANES), jnp.float32),
            jax.ShapeDtypeStruct((rows, ROW_GROUP * kv_cache.shape[1]), jnp.float32),
            *messages,
        ],
        in_specs=[HBM] * len(operands),
        out_specs=[VMEM] * (2 + len(messages)),
        scratch_shapes=[
            pltpu.SMEM(block_adapter.shape, jnp.int32),
            pltpu.SMEM(block_fill.shape, jnp.int32),
            pltpu.SMEM(cache_len.shape, jnp.int32),
            pltpu.VMEM((groups, cols, LANES), jnp.bfloat16),
            pltpu.SemaphoreType.DMA((3,)),
            pltpu.SemaphoreType.DMA((groups,)),
            pltpu.SemaphoreType.DMA((groups,)),
        ],
        compiler_params=pltpu.CompilerParams(vmem_limit_bytes=4 << 20),
        name="pack",
    )(*(pltpu.with_memory_space_constraint(x, pltpu.HBM) for x in operands))


def base_kernel(hidden_ref, head_ref, weight_hbm, base_ref, tail_ref, tail_sem):
    steps, rows, _ = hidden_ref.shape
    head = head_ref.shape[0]
    chunks = tail_sem.shape[0]

    def tail(i):
        at = pl.multiple_of(i * CHUNK, CHUNK)
        source = weight_hbm.at[pl.ds(pl.multiple_of(head + i * CHUNK, CHUNK), CHUNK)]
        return pltpu.make_async_copy(source, tail_ref.at[pl.ds(at, CHUNK)], tail_sem.at[i])

    for i in range(chunks):
        tail(i).start()
    states = hidden_ref[:, :, :head].reshape(steps * rows, head)
    base_ref[...] = jnp.dot(states, head_ref[...], preferred_element_type=jnp.float32)

    def step(i, carry):
        tail(i).wait()
        states = hidden_ref[:, :, pl.ds(pl.multiple_of(head + i * CHUNK, CHUNK), CHUNK)]
        part = tail_ref[pl.ds(pl.multiple_of(i * CHUNK, CHUNK), CHUNK), :]
        base_ref[...] += jnp.dot(states.reshape(steps * rows, CHUNK), part, preferred_element_type=jnp.float32)
        return carry

    lax.fori_loop(0, chunks, step, 0)


def base_projection(hidden, head, kv_weight):
    steps, rows, width = hidden.shape
    cols = kv_weight.shape[1]
    chunks = (width - head.shape[0]) // CHUNK
    return pl.pallas_call(
        base_kernel,
        out_shape=jax.ShapeDtypeStruct((steps * rows, cols), jnp.float32),
        in_specs=[VMEM, VMEM, HBM],
        out_specs=VMEM,
        scratch_shapes=[
            pltpu.VMEM((chunks * CHUNK, cols), kv_weight.dtype),
            pltpu.SemaphoreType.DMA((chunks,)),
        ],
        cost_estimate=pl.CostEstimate(
            flops=2 * steps * rows * width * cols,
            bytes_accessed=2 * width * cols + 2 * steps * rows * width,
            transcendentals=0,
        ),
        compiler_params=pltpu.CompilerParams(vmem_limit_bytes=14 << 20),
        name="base",
    )(hidden, head, pltpu.with_memory_space_constraint(kv_weight, pltpu.HBM))


def cache_kernel(bias_ref, query_ref, cache_ref, weight_hbm, mix_ref, sum_ref, max_ref, head_ref, head_sem):
    head_copy = pltpu.make_async_copy(weight_hbm.at[pl.ds(0, head_ref.shape[0])], head_ref, head_sem)
    head_copy.start()
    steps, rows, _ = query_ref.shape
    positions = cache_ref.shape[1]
    kv_heads = cache_ref.shape[2] // (2 * HEAD)
    share = query_ref.shape[2] // (kv_heads * HEAD)
    wide = ROW_GROUP * positions
    ones = jnp.ones((wide, HEAD), jnp.bfloat16)

    def pair(p, carry):
        first = pl.multiple_of(p * 2 * ROW_GROUP, 2 * ROW_GROUP)
        for half in range(2):
            own = pl.ds(pl.multiple_of(first + half * ROW_GROUP, ROW_GROUP), ROW_GROUP)
            bias = bias_ref[own, :]
            for g in range(kv_heads):
                stored = cache_ref[own, :, g * 2 * HEAD : (g + 1) * 2 * HEAD].reshape(wide, 2 * HEAD)
                parts = []
                for s in range(steps):
                    for j in range(share):
                        at = (g * share + j) * HEAD
                        both = query_ref[s, pl.ds(first, 2 * ROW_GROUP), at : at + HEAD]
                        both = both.astype(jnp.float32)
                        parts.append(both[half * ROW_GROUP : (half + 1) * ROW_GROUP])
                stacked = jnp.concatenate(parts, axis=0).astype(jnp.bfloat16)
                scores = dot_t(stacked, stored[:, :HEAD]).reshape(steps * share, ROW_GROUP, wide)
                scores = scores + bias[None]
                highest = jnp.max(scores, axis=-1, keepdims=True)
                weights = jnp.exp2((scores - highest) * EXP_SCALE).reshape(-1, wide).astype(jnp.bfloat16)
                values = jnp.concatenate([stored[:, HEAD:], ones], axis=1)
                mixed = jnp.dot(weights, values, preferred_element_type=jnp.float32)
                mixed = mixed.reshape(steps, share, ROW_GROUP, 2 * HEAD)
                mix_ref[g, :, :, own, :] = mixed[..., :HEAD]
                sum_ref[g, :, :, own, :] = mixed[..., HEAD:]
                max_ref[g, :, :, own, :] = jnp.broadcast_to(
                    highest.reshape(steps, share, ROW_GROUP, 1), (steps, share, ROW_GROUP, HEAD)
                )
        return carry

    lax.fori_loop(0, rows // (2 * ROW_GROUP), pair, 0)
    head_copy.wait()


def cache_attention(bias, query, kv_cache, kv_weight):
    steps, rows, heads_width = query.shape
    kv_heads = kv_cache.shape[2] // (2 * HEAD)
    share = heads_width // (kv_heads * HEAD)
    head = jax.ShapeDtypeStruct((HEAD_CHUNKS * CHUNK, kv_weight.shape[1]), kv_weight.dtype)
    shape = jax.ShapeDtypeStruct((kv_heads, steps, share, rows, HEAD), jnp.float32)
    return pl.pallas_call(
        cache_kernel,
        out_shape=[shape] * 3 + [head],
        in_specs=[VMEM] * 3 + [HBM],
        out_specs=[VMEM] * 4,
        scratch_shapes=[pltpu.SemaphoreType.DMA],
        cost_estimate=pl.CostEstimate(
            flops=40 * 2 * 2 * steps * heads_width * rows * ROW_GROUP * kv_cache.shape[1],
            bytes_accessed=2 * kv_cache.size,
            transcendentals=0,
        ),
        compiler_params=pltpu.CompilerParams(vmem_limit_bytes=12 << 20),
        name="cached",
    )(bias, query, kv_cache, pltpu.with_memory_space_constraint(kv_weight, pltpu.HBM))


def pieces(groups, size):
    return [(e, d, ((groups == 2 and e == 1) != (d > 0))) for d in range(size) for e in range(groups)]


def piece_source(groups, size, e, d):
    me = lax.axis_index("serve")
    first = me // size if groups == 2 else 0
    return lax.rem(first + e, groups) * size + (lax.rem(me, size) ^ d)


def shrink_kernel(groups, size, cols, hidden_ref, *rest):
    part_refs, (send_ref, up_ref) = rest[:-2], rest[-2:]
    steps, rows, _ = hidden_ref.shape
    total = steps * rows
    width = (part_refs[0].shape[1] - LANES) // groups
    sums = [jnp.zeros((total, RANK), jnp.float32)] * 2
    at = 2 * total
    for e, d, crossed in pieces(groups, size):
        source = piece_source(groups, size, e, d)
        states = hidden_ref[:, :, pl.ds(pl.multiple_of(source * width, LANES), width)]
        factors = part_refs[d][:, e * width : (e + 1) * width]
        sums[crossed] = sums[crossed] + dot_t(states.reshape(total, width), factors)
        shift = lax.rem((lax.rem(source, LANES // cols) - e) * cols + LANES, LANES)
        up = pltpu.roll(part_refs[d][:, groups * width :].astype(jnp.float32), shift, 1)
        if crossed:
            send_ref[at : at + RANK, :] = up
            at += RANK
        else:
            up_ref[source] = up.astype(jnp.bfloat16)
    send_ref[:total, :RANK] = sums[0]
    send_ref[total : 2 * total, :RANK] = sums[1]


def shrink(hidden, parts, groups, size, cols):
    steps, rows, _ = hidden.shape
    crossed = sum(c for _, _, c in pieces(groups, size))
    return pl.pallas_call(
        functools.partial(shrink_kernel, groups, size, cols),
        out_shape=[
            jax.ShapeDtypeStruct((2 * steps * rows + crossed * RANK, LANES), jnp.float32),
            jax.ShapeDtypeStruct((groups * size, RANK, LANES), jnp.bfloat16),
        ],
        in_specs=[VMEM] * (1 + len(parts)),
        out_specs=[VMEM] * 2,
        compiler_params=pltpu.CompilerParams(vmem_limit_bytes=4 << 20),
        name="shrink",
    )(hidden, *parts)


def final_kernel(
    groups, size, cols, live_ref, sent_ref, came_ref, straight_ref, base_ref, query_ref, mix_ref, sum_ref, max_ref,
    new_hbm, attn_hbm, up_ref, new_ref, attn_ref, out_sem,
):
    steps, rows, _ = query_ref.shape
    kv_heads, _, share = mix_ref.shape[:3]
    total = steps * rows
    live = live_ref[...]
    core = lax.axis_index("tensor")
    own_sum = sent_ref[:total, :RANK] + came_ref[total : 2 * total, :RANK]
    other_sum = sent_ref[total : 2 * total, :RANK] + came_ref[:total, :RANK]
    keys_low = (live[:, :RANK] * jnp.where(core == 0, own_sum, other_sum)).astype(jnp.bfloat16)
    values_low = (live[:, :RANK] * jnp.where(core == 0, other_sum, own_sum)).astype(jnp.bfloat16)
    at = 2 * total
    for e, d, crossed in pieces(groups, size):
        source = piece_source(groups, size, e, d)
        if crossed:
            up_ref[source] = came_ref[at : at + RANK, :].astype(jnp.bfloat16)
            at += RANK
        else:
            up_ref[source] = straight_ref[source]
    lane = lax.broadcasted_iota(jnp.int32, (RANK, LANES), 1)
    each = LANES // cols
    query_row = lax.broadcasted_iota(jnp.int32, (total, total), 0)
    key_row = lax.broadcasted_iota(jnp.int32, (total, total), 1)
    seen = (query_row % rows == key_row % rows) & (key_row // rows <= query_row // rows)
    bias = jnp.where(seen, 0.0, -jnp.inf).reshape(steps, 1, rows, total)
    ones = jnp.ones((total, HEAD), jnp.bfloat16)
    live_row = live[:rows]
    fresh = []
    for tile in range(2 * kv_heads):
        up = up_ref[tile * each]
        for k in range(1, each):
            up = jnp.where(lane // cols == k, up_ref[tile * each + k], up)
        low = keys_low if tile % 2 == 0 else values_low
        delta = jnp.dot(low, up, preferred_element_type=jnp.float32)
        at = slice(tile * HEAD, (tile + 1) * HEAD)
        value = (live * (base_ref[:, at] + ADAPTER_SCALE * delta)).astype(jnp.bfloat16)
        new_ref[:, :, at] = value.reshape(steps, rows, HEAD)
        fresh.append(value)
    copies = [pltpu.make_async_copy(new_ref, new_hbm, out_sem.at[0])]
    copies[0].start()
    todo = [(g, s) for g in range(kv_heads) for s in range(steps)]
    found = []
    for g, s in todo:
        queries = jnp.concatenate(
            [query_ref[s, :, (g * share + j) * HEAD : (g * share + j + 1) * HEAD] for j in range(share)], axis=0
        )
        scores = dot_t(queries, fresh[2 * g]).reshape(share, rows, total) + bias[s]
        found.append((scores, jnp.max(scores, axis=-1, keepdims=True)))
    for (g, s), (scores, most) in zip(todo, found):
        cached_max = max_ref[g, s]
        highest = jnp.maximum(cached_max, most)
        weights = jnp.exp2((scores - highest[:, :, :total]) * EXP_SCALE)
        keep = jnp.exp2((cached_max - highest) * EXP_SCALE)
        values = jnp.concatenate([fresh[2 * g + 1], ones], axis=1)
        mixed = jnp.dot(
            weights.reshape(-1, total).astype(jnp.bfloat16), values, preferred_element_type=jnp.float32
        ).reshape(share, rows, 2 * HEAD)
        top = mix_ref[g, s] * keep + mixed[..., :HEAD]
        bottom = sum_ref[g, s] * keep + mixed[..., HEAD:]
        result = (top / bottom * live_row[None]).astype(jnp.bfloat16)
        for j in range(share):
            attn_ref[s, :, (g * share + j) * HEAD : (g * share + j + 1) * HEAD] = result[j]
        span = pl.ds(g * share * HEAD, share * HEAD)
        copies.append(
            pltpu.make_async_copy(attn_ref.at[s, :, span], attn_hbm.at[s, :, span], out_sem.at[1 + g * steps + s])
        )
        copies[-1].start()
    for copy in copies:
        copy.wait()


def finish(live, sent, came, up, base, query, cached, groups, size, cols):
    steps, rows, _ = query.shape
    return pl.pallas_call(
        functools.partial(final_kernel, groups, size, cols),
        out_shape=[
            jax.ShapeDtypeStruct((steps, rows, base.shape[1]), jnp.bfloat16),
            jax.ShapeDtypeStruct(query.shape, jnp.bfloat16),
        ],
        in_specs=[VMEM] * 9,
        out_specs=[HBM] * 2,
        scratch_shapes=[
            pltpu.VMEM(up.shape, up.dtype),
            pltpu.VMEM((steps, rows, base.shape[1]), jnp.bfloat16),
            pltpu.VMEM(query.shape, jnp.bfloat16),
            pltpu.SemaphoreType.DMA((1 + steps * cached[0].shape[0],)),
        ],
        compiler_params=pltpu.CompilerParams(vmem_limit_bytes=8 << 20),
        name="finish",
    )(live, sent, came, up, base, query, *cached)


def join(slices, cols):
    run = jnp.arange(LANES)[None, :] // cols
    up = slices[0][:, -LANES:]
    for e, part in enumerate(slices[1:], 1):
        up = jnp.where(run == e, part[:, -LANES:], up)
    return jnp.concatenate([part[:, :-LANES] for part in slices] + [up], axis=1)


def local(
    hidden, query, kv_weight, down_store, up_store, kv_cache, cache_len, block_adapter, block_fill
):
    serve = lax.axis_size("serve")
    rows = hidden.shape[1]
    size = BLK // rows
    groups = serve // size
    both = ("serve", "tensor")

    def crossing(d):
        return [(i * 2 + t, (i ^ d) * 2 + 1 - t) for i in range(serve) for t in range(2)]

    live, bias, *packed = pack(
        block_adapter, block_fill, cache_len, down_store, up_store, query, kv_cache, groups, size
    )
    if groups == 2:
        other, own = packed
        slices = [own, lax.ppermute(other, both, crossing(size))]
    else:
        same = [[g * size + j for g in range(groups)] for j in range(size)]
        slices = list(lax.all_to_all(packed[0], "serve", 0, 0, axis_index_groups=same, tiled=True))
    arrived = join(slices, up_store.shape[1])
    *cached, head = cache_attention(bias, query, kv_cache, kv_weight)
    arrived, cached, head, hidden = lax.optimization_barrier((arrived, cached, head, hidden))
    parts = [arrived]
    for d in range(1, size):
        parts.append(lax.ppermute(arrived, both, crossing(d)))
    base = base_projection(hidden, head, kv_weight)
    parts, base = lax.optimization_barrier((parts, base))
    sent, up = shrink(hidden, parts, groups, size, up_store.shape[1])
    came = lax.ppermute(sent, "tensor", [(0, 1), (1, 0)])
    return tuple(finish(live, sent, came, up, base, query, cached, groups, size, up_store.shape[1]))


def solution(mesh):
    in_specs = (
        P(None, ("parts", "serve"), None),
        P(None, ("parts", "serve"), "tensor"),
        P(None, "tensor"),
        P("tensor", None, "serve"),
        P("tensor", "serve", None),
        P(("parts", "serve"), None, "tensor"),
        P(("parts", "serve")),
        P("parts"),
        P("parts"),
    )
    out_specs = (P(None, ("parts", "serve"), "tensor"), P(None, ("parts", "serve"), "tensor"))
    return jax.shard_map(local, mesh=mesh, in_specs=in_specs, out_specs=out_specs, check_vma=False)
```

```python
import functools
import math

import jax
import jax.numpy as jnp
from jax import lax
from jax.experimental import pallas as pl
from jax.experimental.pallas import tpu as pltpu
from jax.sharding import PartitionSpec as P

HEAD = 128
RANK = 16
BLK = 128
LANES = 128
ADAPTER_SCALE = 2.0
ROW_GROUP = 8
CHUNK = 1024
HEAD_CHUNKS = 3
EXP_SCALE = HEAD ** (-0.5) * math.log2(math.e)

HBM = pl.BlockSpec(memory_space=pl.ANY)
SMEM = pl.BlockSpec(memory_space=pltpu.SMEM)
VMEM = pl.BlockSpec(memory_space=pltpu.VMEM)


def dot_t(a, b):
    return lax.dot_general(a, b, (((1,), (1,)), ((), ())), preferred_element_type=jnp.float32)


def pack_kernel(
    groups, size, positions, ids_ref, fill_ref, len_ref, down_ref, up_ref, live_out, bias_out, *rest,
):
    out_refs, (ids, fill, lengths, window, small_sem, down_sem, up_sem) = rest[:-7], rest[-7:]
    serve = lax.axis_index("serve")
    rows = bias_out.shape[0]
    small = [
        pltpu.make_async_copy(source, target, small_sem.at[k])
        for k, (source, target) in enumerate(((ids_ref, ids), (fill_ref, fill), (len_ref, lengths)))
    ]
    for copy in small:
        copy.start(priority=1)
    small[0].wait()
    first = serve // size if groups == 2 else 0
    width = down_ref.shape[2]
    cols = up_ref.shape[1]
    copies = []
    starts = []
    for k in range(groups):
        adapter = ids[lax.rem(first + groups - 1 + k, groups)]
        out = out_refs[k] if groups == 2 else out_refs[0].at[(groups - 1 + k) % groups]
        down = pltpu.make_async_copy(
            down_ref.at[0, pl.ds(pl.multiple_of(adapter * RANK, RANK), RANK), :],
            out.at[:, pl.ds(0, width)],
            down_sem.at[k],
        )
        lane = adapter * RANK // LANES * LANES
        up = pltpu.make_async_copy(
            up_ref.at[0, :, pl.ds(pl.multiple_of(lane, LANES), LANES)], window.at[k], up_sem.at[k]
        )
        up.start(priority=1)
        down.start(priority=1)
        copies.append((down, up, out))
        starts.append(adapter * RANK - lane)
    small[1].wait()
    small[2].wait()
    total = live_out.shape[0]
    row = lax.broadcasted_iota(jnp.int32, (total, LANES), 0) % rows + lax.rem(serve, size) * rows
    live_out[...] = (row < fill[serve // size]).astype(jnp.float32)
    wide = bias_out.shape[1]
    lanes = lax.broadcasted_iota(jnp.int32, (ROW_GROUP, wide), 1)
    subs = lax.broadcasted_iota(jnp.int32, (ROW_GROUP, wide), 0)
    start = subs * positions
    for at in range(0, rows, ROW_GROUP):
        used = jnp.zeros((ROW_GROUP, wide), jnp.int32)
        for r in range(ROW_GROUP):
            used = jnp.where(subs == r, lengths[at + r], used)
        bias_out[at : at + ROW_GROUP, :] = jnp.where((lanes >= start) & (lanes < start + used), 0.0, -jnp.inf)
    ranks = lax.broadcasted_iota(jnp.int32, (RANK, LANES), 0)
    lanes = lax.broadcasted_iota(jnp.int32, (RANK, LANES), 1)
    chosen = [(lanes == ranks + start).astype(jnp.bfloat16) for start in starts]
    for _, up, _ in copies:
        up.wait()
    picked = [dot_t(chosen[k], jnp.concatenate([window[k]] * (LANES // cols), axis=0)) for k in range(groups)]
    for k in range(groups):
        copies[k][2][:, width : width + LANES] = picked[k].astype(jnp.bfloat16)
    for down, _, _ in copies:
        down.wait()


def pack(block_adapter, block_fill, cache_len, down_store, up_store, query, kv_cache, groups, size):
    width = down_store.shape[2] + LANES
    cols = up_store.shape[1]
    steps, rows, _ = query.shape
    if groups == 2:
        messages = [jax.ShapeDtypeStruct((RANK, width), jnp.bfloat16)] * 2
    else:
        messages = [jax.ShapeDtypeStruct((groups, RANK, width), jnp.bfloat16)]
    operands = (block_adapter, block_fill, cache_len, down_store, up_store)
    return pl.pallas_call(
        functools.partial(pack_kernel, groups, size, kv_cache.shape[1]),
        out_shape=[
            jax.ShapeDtypeStruct((steps * rows, LANES), jnp.float32),
            jax.ShapeDtypeStruct((rows, ROW_GROUP * kv_cache.shape[1]), jnp.float32),
            *messages,
        ],
        in_specs=[HBM] * len(operands),
        out_specs=[VMEM] * (2 + len(messages)),
        scratch_shapes=[
            pltpu.SMEM(block_adapter.shape, jnp.int32),
            pltpu.SMEM(block_fill.shape, jnp.int32),
            pltpu.SMEM(cache_len.shape, jnp.int32),
            pltpu.VMEM((groups, cols, LANES), jnp.bfloat16),
            pltpu.SemaphoreType.DMA((3,)),
            pltpu.SemaphoreType.DMA((groups,)),
            pltpu.SemaphoreType.DMA((groups,)),
        ],
        compiler_params=pltpu.CompilerParams(vmem_limit_bytes=4 << 20),
        name="pack",
    )(*(pltpu.with_memory_space_constraint(x, pltpu.HBM) for x in operands))


def base_kernel(hidden_ref, head_ref, weight_hbm, base_ref, tail_ref, tail_sem):
    steps, rows, _ = hidden_ref.shape
    head = head_ref.shape[0]
    chunks = tail_sem.shape[0]

    def tail(i):
        at = pl.multiple_of(i * CHUNK, CHUNK)
        source = weight_hbm.at[pl.ds(pl.multiple_of(head + i * CHUNK, CHUNK), CHUNK)]
        return pltpu.make_async_copy(source, tail_ref.at[pl.ds(at, CHUNK)], tail_sem.at[i])

    for i in range(chunks):
        tail(i).start()
    states = hidden_ref[:, :, :head].reshape(steps * rows, head)
    base_ref[...] = jnp.dot(states, head_ref[...], preferred_element_type=jnp.float32)

    def step(i, carry):
        tail(i).wait()
        states = hidden_ref[:, :, pl.ds(pl.multiple_of(head + i * CHUNK, CHUNK), CHUNK)]
        part = tail_ref[pl.ds(pl.multiple_of(i * CHUNK, CHUNK), CHUNK), :]
        base_ref[...] += jnp.dot(states.reshape(steps * rows, CHUNK), part, preferred_element_type=jnp.float32)
        return carry

    lax.fori_loop(0, chunks, step, 0)


def base_projection(hidden, head, kv_weight):
    steps, rows, width = hidden.shape
    cols = kv_weight.shape[1]
    chunks = (width - head.shape[0]) // CHUNK
    return pl.pallas_call(
        base_kernel,
        out_shape=jax.ShapeDtypeStruct((steps * rows, cols), jnp.float32),
        in_specs=[VMEM, VMEM, HBM],
        out_specs=VMEM,
        scratch_shapes=[
            pltpu.VMEM((chunks * CHUNK, cols), kv_weight.dtype),
            pltpu.SemaphoreType.DMA((chunks,)),
        ],
        cost_estimate=pl.CostEstimate(
            flops=2 * steps * rows * width * cols,
            bytes_accessed=2 * width * cols + 2 * steps * rows * width,
            transcendentals=0,
        ),
        compiler_params=pltpu.CompilerParams(vmem_limit_bytes=14 << 20),
        name="base",
    )(hidden, head, pltpu.with_memory_space_constraint(kv_weight, pltpu.HBM))


def cache_kernel(bias_ref, query_ref, cache_ref, weight_hbm, mix_ref, sum_ref, max_ref, head_ref, head_sem):
    head_copy = pltpu.make_async_copy(weight_hbm.at[pl.ds(0, head_ref.shape[0])], head_ref, head_sem)
    head_copy.start()
    steps, rows, _ = query_ref.shape
    positions = cache_ref.shape[1]
    kv_heads = cache_ref.shape[2] // (2 * HEAD)
    share = query_ref.shape[2] // (kv_heads * HEAD)
    wide = ROW_GROUP * positions
    ones = jnp.ones((wide, HEAD), jnp.bfloat16)

    def pair(p, carry):
        first = pl.multiple_of(p * 2 * ROW_GROUP, 2 * ROW_GROUP)
        for half in range(2):
            own = pl.ds(pl.multiple_of(first + half * ROW_GROUP, ROW_GROUP), ROW_GROUP)
            bias = bias_ref[own, :]
            for g in range(kv_heads):
                stored = cache_ref[own, :, g * 2 * HEAD : (g + 1) * 2 * HEAD].reshape(wide, 2 * HEAD)
                parts = []
                for s in range(steps):
                    for j in range(share):
                        at = (g * share + j) * HEAD
                        both = query_ref[s, pl.ds(first, 2 * ROW_GROUP), at : at + HEAD]
                        both = both.astype(jnp.float32)
                        parts.append(both[half * ROW_GROUP : (half + 1) * ROW_GROUP])
                stacked = jnp.concatenate(parts, axis=0).astype(jnp.bfloat16)
                scores = dot_t(stacked, stored[:, :HEAD]).reshape(steps * share, ROW_GROUP, wide)
                scores = scores + bias[None]
                highest = jnp.max(scores, axis=-1, keepdims=True)
                weights = jnp.exp2((scores - highest) * EXP_SCALE).reshape(-1, wide).astype(jnp.bfloat16)
                values = jnp.concatenate([stored[:, HEAD:], ones], axis=1)
                mixed = jnp.dot(weights, values, preferred_element_type=jnp.float32)
                mixed = mixed.reshape(steps, share, ROW_GROUP, 2 * HEAD)
                mix_ref[g, :, :, own, :] = mixed[..., :HEAD]
                sum_ref[g, :, :, own, :] = mixed[..., HEAD:]
                max_ref[g, :, :, own, :] = jnp.broadcast_to(
                    highest.reshape(steps, share, ROW_GROUP, 1), (steps, share, ROW_GROUP, HEAD)
                )
        return carry

    lax.fori_loop(0, rows // (2 * ROW_GROUP), pair, 0)
    head_copy.wait()


def cache_attention(bias, query, kv_cache, kv_weight):
    steps, rows, heads_width = query.shape
    kv_heads = kv_cache.shape[2] // (2 * HEAD)
    share = heads_width // (kv_heads * HEAD)
    head = jax.ShapeDtypeStruct((HEAD_CHUNKS * CHUNK, kv_weight.shape[1]), kv_weight.dtype)
    shape = jax.ShapeDtypeStruct((kv_heads, steps, share, rows, HEAD), jnp.float32)
    return pl.pallas_call(
        cache_kernel,
        out_shape=[shape] * 3 + [head],
        in_specs=[VMEM] * 3 + [HBM],
        out_specs=[VMEM] * 4,
        scratch_shapes=[pltpu.SemaphoreType.DMA],
        cost_estimate=pl.CostEstimate(
            flops=40 * 2 * 2 * steps * heads_width * rows * ROW_GROUP * kv_cache.shape[1],
            bytes_accessed=2 * kv_cache.size,
            transcendentals=0,
        ),
        compiler_params=pltpu.CompilerParams(vmem_limit_bytes=12 << 20),
        name="cached",
    )(bias, query, kv_cache, pltpu.with_memory_space_constraint(kv_weight, pltpu.HBM))


def pieces(groups, size):
    return [(e, d, ((groups == 2 and e == 1) != (d > 0))) for d in range(size) for e in range(groups)]


def piece_source(groups, size, e, d):
    me = lax.axis_index("serve")
    first = me // size if groups == 2 else 0
    return lax.rem(first + e, groups) * size + (lax.rem(me, size) ^ d)


def shrink_kernel(groups, size, cols, hidden_ref, *rest):
    part_refs, (send_ref, up_ref) = rest[:-2], rest[-2:]
    steps, rows, _ = hidden_ref.shape
    total = steps * rows
    width = (part_refs[0].shape[1] - LANES) // groups
    sums = [jnp.zeros((total, RANK), jnp.float32)] * 2
    at = 2 * total
    for e, d, crossed in pieces(groups, size):
        source = piece_source(groups, size, e, d)
        states = hidden_ref[:, :, pl.ds(pl.multiple_of(source * width, LANES), width)]
        factors = part_refs[d][:, e * width : (e + 1) * width]
        sums[crossed] = sums[crossed] + dot_t(states.reshape(total, width), factors)
        shift = lax.rem((lax.rem(source, LANES // cols) - e) * cols + LANES, LANES)
        up = pltpu.roll(part_refs[d][:, groups * width :].astype(jnp.float32), shift, 1)
        if crossed:
            send_ref[at : at + RANK, :] = up
            at += RANK
        else:
            up_ref[source] = up.astype(jnp.bfloat16)
    send_ref[:total, :RANK] = sums[0]
    send_ref[total : 2 * total, :RANK] = sums[1]


def shrink(hidden, parts, groups, size, cols):
    steps, rows, _ = hidden.shape
    crossed = sum(c for _, _, c in pieces(groups, size))
    return pl.pallas_call(
        functools.partial(shrink_kernel, groups, size, cols),
        out_shape=[
            jax.ShapeDtypeStruct((2 * steps * rows + crossed * RANK, LANES), jnp.float32),
            jax.ShapeDtypeStruct((groups * size, RANK, LANES), jnp.bfloat16),
        ],
        in_specs=[VMEM] * (1 + len(parts)),
        out_specs=[VMEM] * 2,
        compiler_params=pltpu.CompilerParams(vmem_limit_bytes=4 << 20),
        name="shrink",
    )(hidden, *parts)


def final_kernel(
    groups, size, cols, live_ref, sent_ref, came_ref, straight_ref, base_ref, query_ref, mix_ref, sum_ref, max_ref,
    new_ref, attn_ref, up_ref,
):
    steps, rows, _ = query_ref.shape
    kv_heads, _, share = mix_ref.shape[:3]
    total = steps * rows
    live = live_ref[...]
    core = lax.axis_index("tensor")
    own_sum = sent_ref[:total, :RANK] + came_ref[total : 2 * total, :RANK]
    other_sum = sent_ref[total : 2 * total, :RANK] + came_ref[:total, :RANK]
    keys_low = (live[:, :RANK] * jnp.where(core == 0, own_sum, other_sum)).astype(jnp.bfloat16)
    values_low = (live[:, :RANK] * jnp.where(core == 0, other_sum, own_sum)).astype(jnp.bfloat16)
    at = 2 * total
    for e, d, crossed in pieces(groups, size):
        source = piece_source(groups, size, e, d)
        if crossed:
            up_ref[source] = came_ref[at : at + RANK, :].astype(jnp.bfloat16)
            at += RANK
        else:
            up_ref[source] = straight_ref[source]
    lane = lax.broadcasted_iota(jnp.int32, (RANK, LANES), 1)
    each = LANES // cols
    query_row = lax.broadcasted_iota(jnp.int32, (total, total), 0)
    key_row = lax.broadcasted_iota(jnp.int32, (total, total), 1)
    seen = (query_row % rows == key_row % rows) & (key_row // rows <= query_row // rows)
    bias = jnp.where(seen, 0.0, -jnp.inf).reshape(steps, 1, rows, total)
    ones = jnp.ones((total, HEAD), jnp.bfloat16)
    live_row = live[:rows]
    fresh = []
    for tile in range(2 * kv_heads):
        up = up_ref[tile * each]
        for k in range(1, each):
            up = jnp.where(lane // cols == k, up_ref[tile * each + k], up)
        low = keys_low if tile % 2 == 0 else values_low
        delta = jnp.dot(low, up, preferred_element_type=jnp.float32)
        at = slice(tile * HEAD, (tile + 1) * HEAD)
        value = (live * (base_ref[:, at] + ADAPTER_SCALE * delta)).astype(jnp.bfloat16)
        new_ref[:, :, at] = value.reshape(steps, rows, HEAD)
        fresh.append(value)
    todo = [(g, s) for g in range(kv_heads) for s in range(steps)]
    found = []
    for g, s in todo:
        queries = jnp.concatenate(
            [query_ref[s, :, (g * share + j) * HEAD : (g * share + j + 1) * HEAD] for j in range(share)], axis=0
        )
        scores = dot_t(queries, fresh[2 * g]).reshape(share, rows, total) + bias[s]
        found.append((scores, jnp.max(scores, axis=-1, keepdims=True)))
    for (g, s), (scores, most) in zip(todo, found):
        cached_max = max_ref[g, s]
        highest = jnp.maximum(cached_max, most)
        weights = jnp.exp2((scores - highest[:, :, :total]) * EXP_SCALE)
        keep = jnp.exp2((cached_max - highest) * EXP_SCALE)
        values = jnp.concatenate([fresh[2 * g + 1], ones], axis=1)
        mixed = jnp.dot(
            weights.reshape(-1, total).astype(jnp.bfloat16), values, preferred_element_type=jnp.float32
        ).reshape(share, rows, 2 * HEAD)
        top = mix_ref[g, s] * keep + mixed[..., :HEAD]
        bottom = sum_ref[g, s] * keep + mixed[..., HEAD:]
        result = (top / bottom * live_row[None]).astype(jnp.bfloat16)
        for j in range(share):
            attn_ref[s, :, (g * share + j) * HEAD : (g * share + j + 1) * HEAD] = result[j]


def finish(live, sent, came, up, base, query, cached, groups, size, cols):
    steps, rows, _ = query.shape
    return pl.pallas_call(
        functools.partial(final_kernel, groups, size, cols),
        out_shape=[
            jax.ShapeDtypeStruct((steps, rows, base.shape[1]), jnp.bfloat16),
            jax.ShapeDtypeStruct(query.shape, jnp.bfloat16),
        ],
        in_specs=[VMEM] * 9,
        out_specs=[VMEM] * 2,
        scratch_shapes=[pltpu.VMEM(up.shape, up.dtype)],
        compiler_params=pltpu.CompilerParams(vmem_limit_bytes=8 << 20),
        name="finish",
    )(live, sent, came, up, base, query, *cached)


def join(slices, cols):
    run = jnp.arange(LANES)[None, :] // cols
    up = slices[0][:, -LANES:]
    for e, part in enumerate(slices[1:], 1):
        up = jnp.where(run == e, part[:, -LANES:], up)
    return jnp.concatenate([part[:, :-LANES] for part in slices] + [up], axis=1)


def local(
    hidden, query, kv_weight, down_store, up_store, kv_cache, cache_len, block_adapter, block_fill
):
    serve = lax.axis_size("serve")
    rows = hidden.shape[1]
    size = BLK // rows
    groups = serve // size
    both = ("serve", "tensor")

    def crossing(d):
        return [(i * 2 + t, (i ^ d) * 2 + 1 - t) for i in range(serve) for t in range(2)]

    live, bias, *packed = pack(
        block_adapter, block_fill, cache_len, down_store, up_store, query, kv_cache, groups, size
    )
    if groups == 2:
        other, own = packed
        slices = [own, lax.ppermute(other, both, crossing(size))]
    else:
        same = [[g * size + j for g in range(groups)] for j in range(size)]
        slices = list(lax.all_to_all(packed[0], "serve", 0, 0, axis_index_groups=same, tiled=True))
    arrived = join(slices, up_store.shape[1])
    *cached, head = cache_attention(bias, query, kv_cache, kv_weight)
    arrived, cached, head, hidden = lax.optimization_barrier((arrived, cached, head, hidden))
    parts = [arrived]
    for d in range(1, size):
        parts.append(lax.ppermute(arrived, both, crossing(d)))
    base = base_projection(hidden, head, kv_weight)
    parts, base = lax.optimization_barrier((parts, base))
    sent, up = shrink(hidden, parts, groups, size, up_store.shape[1])
    came = lax.ppermute(sent, "tensor", [(0, 1), (1, 0)])
    return tuple(finish(live, sent, came, up, base, query, cached, groups, size, up_store.shape[1]))


def solution(mesh):
    in_specs = (
        P(None, ("parts", "serve"), None),
        P(None, ("parts", "serve"), "tensor"),
        P(None, "tensor"),
        P("tensor", None, "serve"),
        P("tensor", "serve", None),
        P(("parts", "serve"), None, "tensor"),
        P(("parts", "serve")),
        P("parts"),
        P("parts"),
    )
    out_specs = (P(None, ("parts", "serve"), "tensor"), P(None, ("parts", "serve"), "tensor"))
    return jax.shard_map(local, mesh=mesh, in_specs=in_specs, out_specs=out_specs, check_vma=False)
```
